32 devices in a mesh: bx: 8 (over z, x), by: 4 (over y, core).
Axes of the slice: x: 2, y: 2, z: 4, core: 2. Of those that a mesh axis runs over, the one named last changes fastest.
Arguments:
- brick_ids: int32 [4096, 3], P(('bx', 'by')), may hold values from 0 to 63, all different within a row; in each aligned block of 128 rows (0 to 127, 128 to 255, ...) at most 18 rows name the same one
- cell_index: int32 [6, 3, 3, 4096], P(None, None, None, ('bx', 'by')), may hold values from 0 to 14
- cell_frac: float32 [6, 3, 3, 4096], P(None, None, None, ('bx', 'by')), may hold values from 0 to 1
- step_length: float32 [3, 3, 4096], P(None, None, ('bx', 'by')), may hold values from 0.01 to 0.05
- target: float32 [3, 4096], P(None, ('bx', 'by')), may hold values from 0 to 1
- planes: bfloat16 [64, 3, 256, 128], P(('bx', 'by')), may hold values from -6 to 6
- first_layer: bfloat16 [64, 128, 256], P(('bx', 'by')), may hold values from -0.5 to 0.5
- last_layer: bfloat16 [64, 4, 256], P(('bx', 'by')), may hold values from -0.375 to 0.375
Outputs:
- colour: float32 [3, 4096], P(None, ('bx', 'by'))
- plane_grad: float32 [64, 3, 256, 128], P(('bx', 'by'))
- first_grad: float32 [64, 128, 256], P(('bx', 'by'))
- last_grad: float32 [64, 4, 256], P(('bx', 'by'))
The draws below stay inside these ranges and needn't reach their ends.
Inputs may be any that keep to these rules, and one draw needn't show every extreme that they name: `brick_ids`: row r lists the 3 different bricks that ray r crosses, in the order in which it crosses them; among the rays of one device no brick is named more than 18 times.
All inputs are finite; a program needn't handle non-finite values.
Results may differ from the reference program's by a relative error of at most 0.007.
The reference program's roundings to bfloat16 on the way count: a program that leaves them out, or rounds other values in their place, can miss the bound.
Values sent between devices are 32-bit elements; how exact they have to be, the bound alone decides.
A program may use at most 64 MiB of HBM per device.

```python
import math
import jax
import jax.numpy as jnp
import numpy as np
from jax import lax

RES = 16
CH = 128
HID = 256
SEG = 3
SAMP = 3
RAY_DEV = 128
BRICKS = 64
RAYS = 4096
CAP = 18
N_BX = 8
N_BY = 4


def touch_ends(array, key, least, top_value):
    index_at = [jax.random.randint(jax.random.fold_in(key, axis), (), 0, length) for axis, length in enumerate(array.shape)]
    main_axis = array.shape.index(max(array.shape))
    neighbour = index_at[:main_axis] + [(index_at[main_axis] + 1) % array.shape[main_axis]] + index_at[main_axis + 1:]
    return array.at[tuple(index_at)].set(least).at[tuple(neighbour)].set(top_value)


def shard_levels(key, dims, cuts, least, largest):
    gain, own = 1.0, jax.random.fold_in(key, 6)
    for axis_at, parts in cuts:
        heights = jnp.exp(jax.random.uniform(jax.random.fold_in(own, axis_at), (parts,), jnp.float32, least / len(cuts), largest / len(cuts)))
        gain = gain * jnp.repeat(heights, dims[axis_at] // parts).reshape([-1 if axis == axis_at else 1 for axis in range(len(dims))])
    return gain


def routed_block(own_key, own, number, rows, number_of, top, limit, lean):
    order = jax.random.permutation(own_key, number_of)
    heavy_load, common = portions_of(number_of, rows * top, limit, lean, True), portions_of(number_of, rows * top, limit, lean, False)
    places = jnp.arange(number_of)

    def named(lengths, offset_by):
        used = int((lengths > 0).sum())
        fixed = max(1, used // 4)
        passed = fixed + (places - fixed + offset_by * (used - fixed)) % max(1, number_of - fixed)
        return jnp.zeros((number_of,), jnp.int32).at[order[jnp.where(places < fixed, places, passed)]].set(jnp.asarray(lengths, jnp.int32))

    lengths = jnp.where(number % 4 == 0, named(heavy_load, number // 4), named(common, number - number // 4 - 1))
    mixed = jax.random.permutation(jax.random.fold_in(own, 3), number_of)
    source_of, receiver = mixed[0:number_of // 2 * 2:2], mixed[1:number_of // 2 * 2:2]
    room = jnp.minimum(lengths[source_of] - 1, limit - lengths[receiver]) // 2
    room = jnp.where((source_of == order[0]) | (receiver == order[0]) | (lengths[receiver] == 0), 0, jnp.maximum(room, 0))
    passed = jax.random.randint(jax.random.fold_in(own, 4), (number_of // 2,), 0, 1 << 20) % (room + 1)
    lengths = lengths.at[source_of].add(-passed).at[receiver].add(passed)
    labels = jnp.searchsorted(jnp.cumsum(lengths), jnp.arange(rows * top), side="right").astype(jnp.int32)
    listing = labels.reshape(top, rows).T
    listing = listing[jax.random.permutation(jax.random.fold_in(own, 1), rows)]
    offset_by = jax.random.randint(jax.random.fold_in(own, 2), (rows, 1), 0, top)
    return jnp.take_along_axis(listing, (jnp.arange(top)[None, :] + offset_by) % top, axis=1)


def portions_of(amount, total, limit, lean, full):
    weights = [(1 << 20) // math.isqrt(grade ** lean) + 1 for grade in range(1, amount + 1)]
    largest = limit if full else min(limit, max(-(-total // amount), total * weights[0] // sum(weights)))
    least = 1 if total - largest >= amount - 1 else 0
    counts, rest = [largest] + [least] * (amount - 1), total - largest - least * (amount - 1)
    while rest > 0:
        candidates = [i for i in range(1, amount) if counts[i] < largest] or [i for i in range(1, amount) if counts[i] < limit]
        mass, budget = sum([weights[i] for i in candidates]), rest
        for i in candidates:
            more = min(limit - counts[i], max(1, budget * weights[i] // mass), rest)
            counts[i] = counts[i] + more
            rest = rest - more
    return np.array(counts)


def bell_draw(rng, shape, width, reach, shards=(), kind=jnp.bfloat16):
    level = shard_levels(rng, shape, shards, -0.22, 0.18) if shards else 1.0
    result = jax.random.normal(rng, shape, jnp.float32) * width * level
    return jnp.minimum(jnp.maximum(result, -reach), reach).astype(kind)


def setup_inputs(seed: int = 0) -> dict:
    splits = jax.random.split(jax.random.key(seed), 9)
    brick_ids_keys = jax.random.split(jax.random.fold_in(splits[0], 1), RAYS // RAY_DEV)
    brick_ids_turns = jax.random.permutation(jax.random.fold_in(splits[0], 3), RAYS // RAY_DEV)
    brick_ids = jax.vmap(lambda own, number: routed_block(jax.random.fold_in(splits[0], 2), own, number, RAY_DEV, BRICKS, SEG, CAP, 2))(brick_ids_keys, brick_ids_turns).reshape((RAYS, SEG))
    cell_index = touch_ends(jax.random.randint(splits[1], (6, SEG, SAMP, RAYS), 0, RES - 1), jax.random.fold_in(splits[1], 1), 0, (RES - 1) - 1).astype(jnp.int32)
    cell_frac = jnp.clip(1.0 * jax.random.uniform(splits[2], (6, SEG, SAMP, RAYS), jnp.float32) ** shard_levels(splits[2], (6, SEG, SAMP, RAYS), ((3, 32),), -0.2, 0.2), 0.0, 1.0)
    step_length = jnp.clip(jnp.exp(math.log(0.05) - 1.609438 * jax.random.uniform(splits[3], (SEG, SAMP, RAYS), jnp.float32) ** shard_levels(splits[3], (SEG, SAMP, RAYS), ((2, 32),), -0.2, 0.2)), 0.01, 0.05)
    target = jnp.clip(1.0 * jax.random.uniform(splits[4], (3, RAYS), jnp.float32) ** shard_levels(splits[4], (3, RAYS), ((1, 32),), -0.2, 0.2), 0.0, 1.0)
    planes = bell_draw(splits[5], (BRICKS, 3, RES * RES, CH), 1.0, 6.0, ((0, 32),))
    first_layer = bell_draw(splits[6], (BRICKS, CH, HID), CH ** -0.5, 0.5, ((0, 32),))
    last_layer = bell_draw(splits[7], (BRICKS, 4, HID), HID ** -0.5, 0.375, ((0, 32),))
    return dict(brick_ids=brick_ids, cell_index=cell_index, cell_frac=cell_frac, step_length=step_length, target=target, planes=planes, first_layer=first_layer, last_layer=last_layer)


def render_rays(density, shade, step_length, target):
    ray_total = density.shape[-1]
    optical = (density * step_length).reshape(-1, ray_total)
    colours = shade.reshape(3, -1, ray_total)
    inclusive = jnp.cumsum(optical, axis=0)
    exclusive = jnp.concatenate([jnp.zeros_like(optical[:1]), inclusive[:-1]], axis=0)
    weight = jnp.exp(-exclusive) * (1.0 - jnp.exp(-optical))
    colour = jnp.sum(weight[None] * colours, axis=1)
    residual = colour - target
    shade_dot = jnp.sum(colours * residual[:, None, :], axis=0)
    contrib = weight * shade_dot
    reverse = jnp.cumsum(contrib[::-1], axis=0)[::-1]
    after = jnp.concatenate([reverse[1:], jnp.zeros_like(reverse[:1])], axis=0)
    density_grad = (jnp.exp(-inclusive) * shade_dot - after) * step_length.reshape(-1, ray_total)
    shade_grad = weight[None] * residual[:, None, :]
    return colour, jnp.concatenate([density_grad[None], shade_grad], axis=0)


def corners(cell_a, cell_b, coord_a, coord_b):
    corner_list = []
    for shift_a in (0, 1):
        for shift_b in (0, 1):
            index_a = cell_a + shift_a
            index_b = cell_b + shift_b
            weight_a = jnp.maximum(0.0, 1.0 - jnp.abs(coord_a - index_a.astype(coord_a.dtype)))
            weight_b = jnp.maximum(0.0, 1.0 - jnp.abs(coord_b - index_b.astype(coord_b.dtype)))
            rounded = lax.optimization_barrier((weight_a * weight_b).astype(jnp.bfloat16))
            corner_list.append(((index_a * RES + index_b).astype(jnp.int32), rounded.astype(coord_a.dtype)))
    return corner_list


def brick_state(plane_set, first_weight, last_weight, cell_rows, data_rows):
    plane_data = plane_set.astype(jnp.float32)
    feature = jnp.zeros((data_rows.shape[1], CH), jnp.float32)
    pieces = []
    for orient in range(3):
        for cell_flat, weight in corners(cell_rows[2 * orient], cell_rows[2 * orient + 1], data_rows[2 * orient], data_rows[2 * orient + 1]):
            feature = feature + weight[:, None] * plane_data[orient][cell_flat]
            pieces.append((orient, cell_flat, weight))
    feature = feature.astype(jnp.bfloat16)
    before_relu = jnp.dot(feature, first_weight, preferred_element_type=jnp.float32)
    hidden = jnp.maximum(before_relu, 0.0).astype(jnp.bfloat16)
    raw_out = jnp.dot(hidden, last_weight.T, preferred_element_type=jnp.float32)
    return pieces, feature, before_relu, hidden, raw_out


def reference(brick_ids, cell_index, cell_frac, step_length, target, planes, first_layer, last_layer):
    devices = N_BX * N_BY
    grouped = brick_ids.reshape(devices, RAY_DEV * SEG)
    member = (grouped[:, :, None] == jnp.arange(BRICKS, dtype=jnp.int32)[None, None, :]).astype(jnp.int32)
    ranking = jnp.sum((jnp.cumsum(member, axis=1) - member) * member, axis=2)
    source = jnp.arange(devices, dtype=jnp.int32)[:, None]
    slot_of = ((grouped * devices + source) * CAP + ranking).reshape(RAYS * SEG).astype(jnp.int32)
    slot_total = BRICKS * devices * CAP
    row_total = devices * CAP * SAMP
    coords = cell_index.astype(jnp.float32) + cell_frac
    payload = jnp.concatenate([coords, step_length[None]], axis=0)
    seg_data = payload.transpose(3, 1, 0, 2).reshape(RAYS * SEG, 7, SAMP)
    seg_cells = cell_index.transpose(3, 1, 0, 2).reshape(RAYS * SEG, 6, SAMP)
    slot_data = jnp.zeros((slot_total, 7, SAMP), jnp.float32).at[slot_of].set(seg_data)
    slot_cells = jnp.zeros((slot_total, 6, SAMP), jnp.int32).at[slot_of].set(seg_cells)
    brick_data = slot_data.reshape(BRICKS, devices * CAP, 7, SAMP).transpose(0, 2, 1, 3).reshape(BRICKS, 7, row_total)
    brick_cells = slot_cells.reshape(BRICKS, devices * CAP, 6, SAMP).transpose(0, 2, 1, 3).reshape(BRICKS, 6, row_total)

    def forward_one(inputs):
        plane_set, first_weight, last_weight, cell_rows, data_rows = inputs
        raw_out = brick_state(plane_set, first_weight, last_weight, cell_rows, data_rows)[4]
        return jnp.concatenate([jax.nn.softplus(raw_out[:, 0])[None], jax.nn.sigmoid(raw_out[:, 1:]).T], axis=0)

    results = lax.map(forward_one, (planes, first_layer, last_layer, brick_cells, brick_data))
    slot_results = results.reshape(BRICKS, 4, devices * CAP, SAMP).transpose(0, 2, 1, 3).reshape(slot_total, 4, SAMP)
    seg_results = slot_results[slot_of].reshape(RAYS, SEG, 4, SAMP).transpose(2, 1, 3, 0)
    colour, cotangent = render_rays(seg_results[0], seg_results[1:], step_length, target)
    seg_cot = cotangent.reshape(4, SEG, SAMP, RAYS).transpose(3, 1, 0, 2).reshape(RAYS * SEG, 4, SAMP)
    slot_cot = jnp.zeros((slot_total, 4, SAMP), jnp.float32).at[slot_of].set(seg_cot)
    brick_cot = slot_cot.reshape(BRICKS, devices * CAP, 4, SAMP).transpose(0, 2, 1, 3).reshape(BRICKS, 4, row_total)

    def backward_one(inputs):
        plane_set, first_weight, last_weight, cell_rows, data_rows, cot_rows = inputs
        pieces, feature, before_relu, hidden, raw_out = brick_state(plane_set, first_weight, last_weight, cell_rows, data_rows)
        shade = jax.nn.sigmoid(raw_out[:, 1:]).T
        raw_grad = jnp.concatenate([(cot_rows[0] * jax.nn.sigmoid(raw_out[:, 0]))[None], cot_rows[1:] * shade * (1.0 - shade)], axis=0).astype(jnp.bfloat16)
        last_part = jnp.dot(raw_grad, hidden, preferred_element_type=jnp.float32)
        hidden_grad = jnp.dot(raw_grad.T, last_weight, preferred_element_type=jnp.float32)
        pre_grad = jnp.where(before_relu > 0, hidden_grad, 0.0).astype(jnp.bfloat16)
        first_part = jnp.dot(feature.T, pre_grad, preferred_element_type=jnp.float32)
        feature_bf = lax.optimization_barrier(jnp.dot(pre_grad, first_weight.T, preferred_element_type=jnp.float32).astype(jnp.bfloat16))
        feature_grad = feature_bf.astype(jnp.float32)
        plane_part = jnp.zeros((3, RES * RES, CH), jnp.float32)
        for orient, cell_flat, weight in pieces:
            plane_part = plane_part.at[orient, cell_flat].add(weight[:, None] * feature_grad)
        return plane_part, first_part, last_part

    plane_grad, first_grad, last_grad = lax.map(backward_one, (planes, first_layer, last_layer, brick_cells, brick_data, brick_cot))
    return colour, plane_grad, first_grad, last_grad
```

```python
import functools

import jax
import jax.numpy as jnp
from jax import lax
from jax.experimental import pallas as pl
from jax.experimental.pallas import tpu as pltpu
from jax.sharding import PartitionSpec as P

MESH = pl.DeviceIdType.MESH
F32 = jnp.float32
BF16 = jnp.bfloat16
LANES = 128
ROWS = 8
GROUP = 8


def matmul(lhs, rhs, contract):
    return lax.dot_general(lhs, rhs, (contract, ((), ())), preferred_element_type=F32)


def exact_parts(value):
    high = value.astype(BF16).astype(F32)
    rest = value - high
    middle = rest.astype(BF16).astype(F32)
    return high, middle, rest - middle


def pair_merge(even, odd, low_lanes):
    half = LANES // 2
    first = jnp.where(low_lanes, even, pltpu.roll(odd, half, 1))
    second = jnp.where(low_lanes, pltpu.roll(even, half, 1), odd)
    return first, second


def step_kernel(
    along_x, along_y, capacity,
    ids_ref, cell_ref, frac_ref, step_ref, target_ref, planes_ref, first_ref, last_ref,
    colour_ref, plane_grad_ref, first_grad_ref, last_grad_ref,
    payload, target_tile, last_wide,
    out_a, in_a, out_b, in_b, out_c, in_c,
    planes_t, first_t, corner, feature, hidden, slope, last_total,
    send_sem, recv_sem,
):
    count = along_x * along_y
    bricks, orients, cells, channels = planes_ref.shape
    side = 1
    while side * side < cells:
        side = side * 2
    crossed, samples, rays = step_ref.shape
    points = crossed * samples
    total = points * rays
    segments = crossed * rays
    half = LANES // bricks
    all_bricks = bricks * count
    chunk = GROUP * half
    chunks = count // GROUP
    me = lax.axis_index("bx") * along_y + lax.axis_index("by")

    def device(number):
        return (lax.div(number, along_y), lax.rem(number, along_y))

    def ahead(offset):
        return device(lax.rem(me + offset, count))

    def behind(offset):
        return device(lax.rem(me + count - offset, count))

    def transfer(phase, source, landing, offset, peer):
        return pltpu.make_async_remote_copy(
            src_ref=source.at[offset],
            dst_ref=landing.at[offset],
            send_sem=send_sem.at[phase, offset],
            recv_sem=recv_sem.at[phase, offset],
            device_id=peer,
            device_id_type=MESH,
        )

    barrier = pltpu.get_barrier_semaphore()

    def greet(offset, carry):
        pl.semaphore_signal(barrier, inc=1, device_id=ahead(offset), device_id_type=MESH)
        return carry

    lax.fori_loop(1, count, greet, 0)

    ids = [ids_ref[pl.ds(k, 1), :] for k in range(crossed)]
    ids_row = jnp.concatenate(ids, axis=1)
    member = lax.broadcasted_iota(jnp.int32, (all_bricks, segments), 0) == ids_row
    member_f = jnp.where(member, 1.0, 0.0).astype(F32)
    earlier = lax.broadcasted_iota(jnp.int32, (segments, segments), 0) < lax.broadcasted_iota(
        jnp.int32, (segments, segments), 1
    )
    ranks = matmul(
        member_f.astype(BF16), jnp.where(earlier, 1.0, 0.0).astype(BF16), ((1,), (0,))
    )
    ranking = jnp.sum(member_f * ranks, axis=0, keepdims=True).astype(jnp.int32)
    shift = bricks.bit_length() - 1
    away = lax.shift_right_logical(ids_row, shift) - me
    away = jnp.where(away < 0, away + count, away)
    place = (ids_row & (bricks - 1)) * half + ranking
    away_all, place_all = [], []
    for k in range(crossed):
        block = slice(k * rays, (k + 1) * rays)
        for s in range(samples):
            away_all.append(away[:, block])
            place_all.append(place[:, block] + s * capacity)
    away_all = jnp.concatenate(away_all, axis=1)
    place_all = jnp.concatenate(place_all, axis=1)
    lane_hot = jnp.where(
        lax.broadcasted_iota(jnp.int32, (LANES, total), 0) == place_all, 1.0, 0.0
    ).astype(BF16)
    chosen = lax.broadcasted_iota(jnp.int32, (count, ROWS, total), 0) == away_all[None]

    def scatter(value):
        tiles = jnp.zeros((count * ROWS, LANES), F32)
        for part in exact_parts(value):
            spread = jnp.where(chosen, part[None], 0.0).reshape(count * ROWS, total).astype(BF16)
            tiles = tiles + matmul(spread, lane_hot, ((1,), (1,)))
        return tiles.reshape(count, ROWS, LANES)

    payload[...] = jnp.zeros_like(payload)
    for k in range(crossed):
        for s in range(samples):
            lanes = pl.ds((k * samples + s) * rays, rays)
            for axis in range(2 * orients):
                payload[pl.ds(axis, 1), lanes] = (
                    cell_ref[axis, k, pl.ds(s, 1), :].astype(F32)
                    + frac_ref[axis, k, pl.ds(s, 1), :]
                )
    tiles = scatter(payload[...])
    out_a[...] = tiles
    in_a[0] = tiles[0]

    pl.semaphore_wait(barrier, count - 1)

    def send_a(offset, carry):
        transfer(0, out_a, in_a, offset, ahead(offset)).start()
        return carry

    lax.fori_loop(1, count, send_a, 0)

    for b in range(bricks):
        for orient in range(orients):
            planes_t[b, :, pl.ds(orient * cells, cells)] = planes_ref[b, orient].T
        first_t[b] = first_ref[b].T
    last_wide[...] = jnp.zeros_like(last_wide)
    for b in range(bricks):
        last_wide[b, pl.ds(0, 4), :] = last_ref[b].astype(F32)
    target_tile[...] = jnp.zeros_like(target_tile)
    target_tile[pl.ds(1, 3), :] = target_ref[...]

    low_lanes = lax.broadcasted_iota(jnp.int32, (ROWS, LANES), 1) < half
    row = lax.broadcasted_iota(jnp.int32, (ROWS, LANES), 0)
    lines = lax.broadcasted_iota(jnp.int32, (side, chunk), 0).astype(F32)
    chunk_row = lax.broadcasted_iota(jnp.int32, (ROWS, chunk), 0)

    def arrive(phase, source, landing, peer, start):
        def wait(offset, carry):
            transfer(phase, source, landing, offset, peer(offset)).wait_recv()
            return carry

        lax.fori_loop(jnp.maximum(start, 1), start + GROUP, wait, 0)

    def split_bricks(landing, start):
        held = [[] for _ in range(bricks)]
        for pair in range(GROUP // 2):
            merged = pair_merge(
                landing[start + 2 * pair], landing[start + 2 * pair + 1], low_lanes
            )
            for b in range(bricks):
                held[b].append(merged[b])
        return [jnp.concatenate(part, axis=1) for part in held]

    def forward(step, carry):
        start = step * GROUP
        lanes = pl.ds(pl.multiple_of(step * chunk, chunk), chunk)
        arrive(0, out_a, in_a, ahead, start)
        spots = split_bricks(in_a, start)
        answers = []
        for b in range(bricks):
            for orient in range(orients):
                near_a = jnp.maximum(
                    0.0, 1.0 - jnp.abs(spots[b][2 * orient : 2 * orient + 1] - lines)
                )
                near_b = jnp.maximum(
                    0.0, 1.0 - jnp.abs(spots[b][2 * orient + 1 : 2 * orient + 2] - lines)
                )
                weights = near_a[:, None, :] * near_b[None, :, :]
                corner[b, pl.ds(orient * cells, cells), lanes] = weights.reshape(
                    cells, chunk
                ).astype(BF16)
            mixed = matmul(planes_t[b], corner[b, :, lanes], ((1,), (0,))).astype(BF16)
            feature[b, :, lanes] = mixed
            before = matmul(first_t[b], mixed, ((1,), (0,)))
            active = jnp.maximum(before, 0.0).astype(BF16)
            hidden[b, :, lanes] = active
            raw = matmul(last_wide[b].astype(BF16), active, ((1,), (0,)))
            gate = jax.nn.sigmoid(raw)
            soft = jnp.maximum(raw, 0.0) + jnp.log1p(jnp.exp(-jnp.abs(raw)))
            answers.append(jnp.where(chunk_row == 0, soft, gate))
            slope[b, :, lanes] = jnp.where(chunk_row == 0, gate, gate * (1.0 - gate))
        for pair in range(GROUP // 2):
            cut = slice(pair * LANES, (pair + 1) * LANES)
            even, odd = pair_merge(answers[0][:, cut], answers[1][:, cut], low_lanes)
            out_b[start + 2 * pair] = even
            out_b[start + 2 * pair + 1] = odd

        def send_b(offset, inner):
            transfer(1, out_b, in_b, offset, behind(offset)).start()
            return inner

        lax.fori_loop(jnp.maximum(start, 1), start + GROUP, send_b, 0)
        return carry

    lax.fori_loop(0, chunks, forward, 0)
    in_b[0] = out_b[0]

    def wait_b(offset, carry):
        transfer(1, out_b, in_b, offset, behind(offset)).wait_recv()
        return carry

    lax.fori_loop(1, count, wait_b, 0)

    found = jnp.zeros((count * ROWS, total), F32)
    for part in exact_parts(in_b[...].reshape(count * ROWS, LANES)):
        found = found + matmul(part.astype(BF16), lane_hot, ((1,), (0,)))
    found = jnp.sum(
        jnp.where(chosen, found.reshape(count, ROWS, total), 0.0), axis=0
    )
    views = [found[:, i * rays : (i + 1) * rays] for i in range(points)]
    lengths = [
        step_ref[k, pl.ds(s, 1), :] for k in range(crossed) for s in range(samples)
    ]
    running = jnp.zeros((1, rays), F32)
    colour = jnp.zeros((ROWS, rays), F32)
    weights, passed = [], []
    for i in range(points):
        depth = views[i][0:1] * lengths[i]
        weight = jnp.exp(-running) * (1.0 - jnp.exp(-depth))
        running = running + depth
        passed.append(jnp.exp(-running))
        weights.append(weight)
        colour = colour + weight * views[i]
    colour_ref[...] = colour[1:4]
    residual = jnp.where((row >= 1) & (row <= 3), colour - target_tile[...], 0.0)
    behind_sum = jnp.zeros((1, rays), F32)
    cotangents = [None] * points
    for i in reversed(range(points)):
        shade_dot = jnp.sum(views[i] * residual, axis=0, keepdims=True)
        density_cot = (passed[i] * shade_dot - behind_sum) * lengths[i]
        behind_sum = behind_sum + weights[i] * shade_dot
        cotangents[i] = jnp.where(row == 0, density_cot, weights[i] * residual)
    tiles = scatter(jnp.concatenate(cotangents, axis=1))
    out_c[...] = tiles
    in_c[0] = tiles[0]

    def send_c(offset, carry):
        transfer(2, out_c, in_c, offset, ahead(offset)).start()
        return carry

    lax.fori_loop(1, count, send_c, 0)

    plane_grad_ref[...] = jnp.zeros_like(plane_grad_ref)
    first_grad_ref[...] = jnp.zeros_like(first_grad_ref)
    last_total[...] = jnp.zeros_like(last_total)

    def backward(step, carry):
        start = step * GROUP
        lanes = pl.ds(pl.multiple_of(step * chunk, chunk), chunk)
        arrive(2, out_c, in_c, ahead, start)
        pulls = split_bricks(in_c, start)
        for b in range(bricks):
            raw_cot = (pulls[b] * slope[b, :, lanes]).astype(BF16)
            active = hidden[b, :, lanes]
            last_total[b] += matmul(raw_cot, active, ((1,), (1,)))
            pull = matmul(last_wide[b].astype(BF16), raw_cot, ((0,), (0,)))
            before_cot = jnp.where(active.astype(F32) > 0.0, pull, 0.0).astype(BF16)
            first_grad_ref[b] += matmul(feature[b, :, lanes], before_cot, ((1,), (1,)))
            feature_cot = matmul(first_ref[b], before_cot, ((1,), (0,))).astype(BF16)
            for orient in range(orients):
                plane_grad_ref[b, orient] += matmul(
                    corner[b, pl.ds(orient * cells, cells), lanes], feature_cot, ((1,), (1,))
                )
        return carry

    lax.fori_loop(0, chunks, backward, 0)
    for b in range(bricks):
        last_grad_ref[b] = last_total[b, pl.ds(0, 4), :]

    def drain(offset, carry):
        transfer(0, out_a, in_a, offset, ahead(offset)).wait_send()
        transfer(1, out_b, in_b, offset, behind(offset)).wait_send()
        transfer(2, out_c, in_c, offset, ahead(offset)).wait_send()
        return carry

    lax.fori_loop(1, count, drain, 0)


def on_device(
    along_x, along_y,
    brick_ids, cell_index, cell_frac, step_length, target, planes, first_layer, last_layer,
):
    count = along_x * along_y
    bricks, orients, cells, channels = planes.shape
    units = first_layer.shape[2]
    rays, crossed = brick_ids.shape
    samples = step_length.shape[1]
    all_bricks = bricks * count
    capacity = max(2, (3 * rays * crossed + all_bricks - 1) // all_bricks)
    half = LANES // bricks
    assert bricks == 2 and capacity * samples <= half and count % GROUP == 0
    slots = count * half
    total = crossed * samples * rays
    vmem = pl.BlockSpec(memory_space=pltpu.VMEM)
    tile = pltpu.VMEM((count, ROWS, LANES), F32)
    return pl.pallas_call(
        functools.partial(step_kernel, along_x, along_y, capacity),
        out_shape=(
            jax.ShapeDtypeStruct(target.shape, F32),
            jax.ShapeDtypeStruct(planes.shape, F32),
            jax.ShapeDtypeStruct(first_layer.shape, F32),
            jax.ShapeDtypeStruct(last_layer.shape, F32),
        ),
        in_specs=[vmem] * 8,
        out_specs=(vmem,) * 4,
        scratch_shapes=[
            pltpu.VMEM((ROWS, total), F32),
            pltpu.VMEM((ROWS, rays), F32),
            pltpu.VMEM((bricks, ROWS, units), F32),
            tile, tile, tile, tile, tile, tile,
            pltpu.VMEM((bricks, channels, orients * cells), BF16),
            pltpu.VMEM((bricks, units, channels), BF16),
            pltpu.VMEM((bricks, orients * cells, slots), BF16),
            pltpu.VMEM((bricks, channels, slots), BF16),
            pltpu.VMEM((bricks, units, slots), BF16),
            pltpu.VMEM((bricks, ROWS, slots), F32),
            pltpu.VMEM((bricks, ROWS, units), F32),
            pltpu.SemaphoreType.DMA((3, count)),
            pltpu.SemaphoreType.DMA((3, count)),
        ],
        compiler_params=pltpu.CompilerParams(
            collective_id=0, has_side_effects=True, vmem_limit_bytes=56 * 1024 * 1024
        ),
    )(brick_ids.T, cell_index, cell_frac, step_length, target, planes, first_layer, last_layer)


def solution(mesh):
    along_x, along_y = mesh.shape["bx"], mesh.shape["by"]
    return jax.shard_map(
        functools.partial(on_device, along_x, along_y),
        mesh=mesh,
        in_specs=(
            P(("bx", "by"), None),
            P(None, None, None, ("bx", "by")),
            P(None, None, None, ("bx", "by")),
            P(None, None, ("bx", "by")),
            P(None, ("bx", "by")),
            P(("bx", "by"), None, None, None),
            P(("bx", "by"), None, None),
            P(("bx", "by"), None, None),
        ),
        out_specs=(
            P(None, ("bx", "by")),
            P(("bx", "by"), None, None, None),
            P(("bx", "by"), None, None),
            P(("bx", "by"), None, None),
        ),
        check_vma=False,
    )
```

```python
import functools

import jax
import jax.numpy as jnp
from jax import lax
from jax.experimental import pallas as pl
from jax.experimental.pallas import tpu as pltpu
from jax.sharding import PartitionSpec as P

MESH = pl.DeviceIdType.MESH
F32 = jnp.float32
BF16 = jnp.bfloat16
LANES = 128
ROWS = 8
GROUP = 8
HALF = 4


def matmul(lhs, rhs, contract):
    return lax.dot_general(lhs, rhs, (contract, ((), ())), preferred_element_type=F32)


def parts_of(value, number):
    parts = []
    for _ in range(number - 1):
        part = value.astype(BF16).astype(F32)
        parts.append(part)
        value = value - part
    return parts + [value]


def pair_merge(even, odd, low_lanes):
    half = LANES // 2
    first = jnp.where(low_lanes, even, pltpu.roll(odd, half, 1))
    second = jnp.where(low_lanes, pltpu.roll(even, half, 1), odd)
    return first, second


def step_kernel(
    along_x, along_y, capacity,
    ids_ref, cell_ref, frac_ref, step_ref, target_ref, planes_ref, first_ref, last_ref,
    colour_ref, plane_grad_ref, first_grad_ref, last_grad_ref,
    payload, target_tile, last_wide,
    out_a, in_a, out_b, in_b, out_c, in_c,
    planes_t, first_t, corner, feature, hidden, slope, last_total,
    send_sem, recv_sem,
):
    count = along_x * along_y
    bricks, orients, cells, channels = planes_ref.shape
    side = 1
    while side * side < cells:
        side = side * 2
    crossed, samples, rays = step_ref.shape
    points = crossed * samples
    total = points * rays
    segments = crossed * rays
    half = LANES // bricks
    all_bricks = bricks * count
    chunk = GROUP * half
    chunks = count // GROUP
    me = lax.axis_index("bx") * along_y + lax.axis_index("by")

    def device(number):
        return (lax.div(number, along_y), lax.rem(number, along_y))

    def ahead(offset):
        return device(lax.rem(me + offset, count))

    def behind(offset):
        return device(lax.rem(me + count - offset, count))

    def transfer(phase, source, landing, offset, peer):
        return pltpu.make_async_remote_copy(
            src_ref=source.at[offset],
            dst_ref=landing.at[offset],
            send_sem=send_sem.at[phase, offset],
            recv_sem=recv_sem.at[phase, offset],
            device_id=peer,
            device_id_type=MESH,
        )

    barrier = pltpu.get_barrier_semaphore()

    def greet(offset, carry):
        pl.semaphore_signal(barrier, inc=1, device_id=ahead(offset), device_id_type=MESH)
        return carry

    lax.fori_loop(1, count, greet, 0)

    ids = [ids_ref[pl.ds(k, 1), :] for k in range(crossed)]
    ids_row = jnp.concatenate(ids, axis=1)
    member = lax.broadcasted_iota(jnp.int32, (all_bricks, segments), 0) == ids_row
    member_f = jnp.where(member, 1.0, 0.0).astype(F32)
    earlier = lax.broadcasted_iota(jnp.int32, (segments, segments), 0) < lax.broadcasted_iota(
        jnp.int32, (segments, segments), 1
    )
    ranks = matmul(
        member_f.astype(BF16), jnp.where(earlier, 1.0, 0.0).astype(BF16), ((1,), (0,))
    )
    ranking = jnp.sum(member_f * ranks, axis=0, keepdims=True).astype(jnp.int32)
    shift = bricks.bit_length() - 1
    away = lax.shift_right_logical(ids_row, shift) - me
    away = jnp.where(away < 0, away + count, away)
    place = (ids_row & (bricks - 1)) * half + ranking
    away_all, place_all = [], []
    for k in range(crossed):
        block = slice(k * rays, (k + 1) * rays)
        for s in range(samples):
            away_all.append(away[:, block])
            place_all.append(place[:, block] + s * capacity)
    away_all = jnp.concatenate(away_all, axis=1)
    place_all = jnp.concatenate(place_all, axis=1)
    lane_hot = jnp.where(
        lax.broadcasted_iota(jnp.int32, (LANES, total), 0) == place_all, 1.0, 0.0
    ).astype(BF16)
    whole = lax.broadcasted_iota(jnp.int32, (count, ROWS, total), 0) == away_all[None]
    halves_of = (count // 2, ROWS, total)
    paired = (
        2 * lax.broadcasted_iota(jnp.int32, halves_of, 0)
        + lax.shift_right_logical(lax.broadcasted_iota(jnp.int32, halves_of, 1), 2)
    ) == away_all[None]

    def scatter(value, chosen, number):
        tiles = chosen.shape[0]
        height = tiles * ROWS
        spread = jnp.concatenate(
            [
                jnp.where(chosen, part[None], 0.0).reshape(height, total).astype(BF16)
                for part in parts_of(value, number)
            ],
            axis=0,
        )
        placed = matmul(spread, lane_hot, ((1,), (1,)))
        merged = placed[:height]
        for at in range(1, number):
            merged = merged + placed[at * height : (at + 1) * height]
        return merged.reshape(tiles, ROWS, LANES)

    payload[...] = jnp.zeros_like(payload)
    for k in range(crossed):
        for s in range(samples):
            lanes = pl.ds((k * samples + s) * rays, rays)
            for axis in range(2 * orients):
                payload[pl.ds(axis, 1), lanes] = (
                    cell_ref[axis, k, pl.ds(s, 1), :].astype(F32)
                    + frac_ref[axis, k, pl.ds(s, 1), :]
                )
    tiles = scatter(payload[...], whole, 3)
    out_a[...] = tiles
    in_a[0] = tiles[0]

    pl.semaphore_wait(barrier, count - 1)

    def send_a(offset, carry):
        transfer(0, out_a, in_a, offset, ahead(offset)).start()
        return carry

    lax.fori_loop(1, count, send_a, 0)

    for b in range(bricks):
        for orient in range(orients):
            planes_t[b, :, pl.ds(orient * cells, cells)] = planes_ref[b, orient].T
        first_t[b] = first_ref[b].T
    last_wide[...] = jnp.zeros_like(last_wide)
    for b in range(bricks):
        last_wide[b, pl.ds(0, 4), :] = last_ref[b].astype(F32)
    target_tile[...] = jnp.zeros_like(target_tile)
    target_tile[pl.ds(1, 3), :] = target_ref[...]
    target_tile[pl.ds(HALF + 1, 3), :] = target_ref[...]

    low_lanes = lax.broadcasted_iota(jnp.int32, (ROWS, LANES), 1) < half
    row = lax.broadcasted_iota(jnp.int32, (ROWS, LANES), 0)
    lines = lax.broadcasted_iota(jnp.int32, (side, chunk), 0).astype(F32)
    chunk_row = lax.broadcasted_iota(jnp.int32, (ROWS, chunk), 0)

    def arrive(phase, source, landing, peer, start):
        def wait(offset, carry):
            transfer(phase, source, landing, offset, peer(offset)).wait_recv()
            return carry

        lax.fori_loop(jnp.maximum(start, 1), start + GROUP, wait, 0)

    def split_bricks(landing, start):
        held = [[] for _ in range(bricks)]
        for pair in range(GROUP // 2):
            even, odd = landing[start + 2 * pair], landing[start + 2 * pair + 1]
            merged = pair_merge(even, odd, low_lanes[: even.shape[0]])
            for b in range(bricks):
                held[b].append(merged[b])
        return [jnp.concatenate(part, axis=1) for part in held]

    def forward(step, carry):
        start = step * GROUP
        lanes = pl.ds(pl.multiple_of(step * chunk, chunk), chunk)
        arrive(0, out_a, in_a, ahead, start)
        spots = split_bricks(in_a, start)
        answers = []
        for b in range(bricks):
            for orient in range(orients):
                near_a = jnp.maximum(
                    0.0, 1.0 - jnp.abs(spots[b][2 * orient : 2 * orient + 1] - lines)
                )
                near_b = jnp.maximum(
                    0.0, 1.0 - jnp.abs(spots[b][2 * orient + 1 : 2 * orient + 2] - lines)
                )
                weights = near_a[:, None, :] * near_b[None, :, :]
                corner[b, pl.ds(orient * cells, cells), lanes] = weights.reshape(
                    cells, chunk
                ).astype(BF16)
            mixed = matmul(planes_t[b], corner[b, :, lanes], ((1,), (0,))).astype(BF16)
            feature[b, :, lanes] = mixed
            before = matmul(first_t[b], mixed, ((1,), (0,)))
            active = jnp.maximum(before, 0.0).astype(BF16)
            hidden[b, :, lanes] = active
            raw = matmul(last_wide[b].astype(BF16), active, ((1,), (0,)))
            gate = jax.nn.sigmoid(raw)
            soft = jnp.maximum(raw, 0.0) + jnp.log1p(jnp.exp(-jnp.abs(raw)))
            answers.append(jnp.where(chunk_row == 0, soft, gate))
            slope[b, :, lanes] = jnp.where(chunk_row == 0, gate, gate * (1.0 - gate))
        for pair in range(GROUP // 2):
            cut = slice(pair * LANES, (pair + 1) * LANES)
            even, odd = pair_merge(answers[0][:, cut], answers[1][:, cut], low_lanes)
            out_b[start + 2 * pair] = even[:HALF]
            out_b[start + 2 * pair + 1] = odd[:HALF]

        def send_b(offset, inner):
            transfer(1, out_b, in_b, offset, behind(offset)).start()
            return inner

        lax.fori_loop(jnp.maximum(start, 1), start + GROUP, send_b, 0)
        return carry

    lax.fori_loop(0, chunks, forward, 0)
    in_b[0] = out_b[0]

    def wait_b(offset, carry):
        transfer(1, out_b, in_b, offset, behind(offset)).wait_recv()
        return carry

    lax.fori_loop(1, count, wait_b, 0)

    held = jnp.concatenate([in_b[t] for t in range(count)], axis=0)
    found = matmul(
        jnp.concatenate([part.astype(BF16) for part in parts_of(held, 2)], axis=0),
        lane_hot,
        ((1,), (0,)),
    )
    found = (found[: count * HALF] + found[count * HALF :]).reshape(halves_of)
    found = jnp.sum(jnp.where(paired, found, 0.0), axis=0)
    found = found[:HALF] + found[HALF:]
    found = jnp.concatenate([found, found], axis=0)
    views = [found[:, i * rays : (i + 1) * rays] for i in range(points)]
    lengths = [
        step_ref[k, pl.ds(s, 1), :] for k in range(crossed) for s in range(samples)
    ]
    running = jnp.zeros((1, rays), F32)
    colour = jnp.zeros((ROWS, rays), F32)
    weights, passed = [], []
    for i in range(points):
        depth = views[i][0:1] * lengths[i]
        weight = jnp.exp(-running) * (1.0 - jnp.exp(-depth))
        running = running + depth
        passed.append(jnp.exp(-running))
        weights.append(weight)
        colour = colour + weight * views[i]
    colour_ref[...] = colour[1:4]
    residual = jnp.where((row & 3) > 0, colour - target_tile[...], 0.0)
    behind_sum = jnp.zeros((1, rays), F32)
    cotangents = [None] * points
    for i in reversed(range(points)):
        shade_dot = jnp.sum((views[i] * residual)[:HALF], axis=0, keepdims=True)
        density_cot = (passed[i] * shade_dot - behind_sum) * lengths[i]
        behind_sum = behind_sum + weights[i] * shade_dot
        cotangents[i] = jnp.where((row & 3) == 0, density_cot, weights[i] * residual)
    tiles = scatter(jnp.concatenate(cotangents, axis=1), paired, 2)
    for t in range(count):
        out_c[t] = tiles[t // 2, (t % 2) * HALF : (t % 2 + 1) * HALF]
    in_c[0] = out_c[0]

    def send_c(offset, carry):
        transfer(2, out_c, in_c, offset, ahead(offset)).start()
        return carry

    lax.fori_loop(1, count, send_c, 0)

    plane_grad_ref[...] = jnp.zeros_like(plane_grad_ref)
    first_grad_ref[...] = jnp.zeros_like(first_grad_ref)
    last_total[...] = jnp.zeros_like(last_total)

    def backward(step, carry):
        start = step * GROUP
        lanes = pl.ds(pl.multiple_of(step * chunk, chunk), chunk)
        arrive(2, out_c, in_c, ahead, start)
        pulls = split_bricks(in_c, start)
        for b in range(bricks):
            raw_cot = (
                jnp.concatenate([pulls[b], jnp.zeros_like(pulls[b])], axis=0) * slope[b, :, lanes]
            ).astype(BF16)
            active = hidden[b, :, lanes]
            last_total[b] += matmul(raw_cot, active, ((1,), (1,)))
            pull = matmul(last_wide[b].astype(BF16), raw_cot, ((0,), (0,)))
            before_cot = jnp.where(active.astype(F32) > 0.0, pull, 0.0).astype(BF16)
            first_grad_ref[b] += matmul(feature[b, :, lanes], before_cot, ((1,), (1,)))
            feature_cot = matmul(first_ref[b], before_cot, ((1,), (0,))).astype(BF16)
            plane_grad_ref[b] += matmul(corner[b, :, lanes], feature_cot, ((1,), (1,)))
        return carry

    lax.fori_loop(0, chunks, backward, 0)
    for b in range(bricks):
        last_grad_ref[b] = last_total[b, pl.ds(0, 4), :]

    def drain(offset, carry):
        transfer(0, out_a, in_a, offset, ahead(offset)).wait_send()
        transfer(1, out_b, in_b, offset, behind(offset)).wait_send()
        transfer(2, out_c, in_c, offset, ahead(offset)).wait_send()
        return carry

    lax.fori_loop(1, count, drain, 0)


def hand_out(*refs):
    sources, landings, sems = refs[:4], refs[4:8], refs[8]
    copies = [
        pltpu.make_async_copy(source, landing, sems.at[at])
        for at, (source, landing) in enumerate(zip(sources, landings))
    ]
    for copy in copies:
        copy.start()
    for copy in copies:
        copy.wait()


def on_device(
    along_x, along_y,
    brick_ids, cell_index, cell_frac, step_length, target, planes, first_layer, last_layer,
):
    count = along_x * along_y
    bricks, orients, cells, channels = planes.shape
    units = first_layer.shape[2]
    rays, crossed = brick_ids.shape
    samples = step_length.shape[1]
    all_bricks = bricks * count
    capacity = max(2, (3 * rays * crossed + all_bricks - 1) // all_bricks)
    half = LANES // bricks
    assert bricks == 2 and capacity * samples <= half and count % GROUP == 0
    slots = count * half
    total = crossed * samples * rays
    vmem = pl.BlockSpec(memory_space=pltpu.VMEM)
    tile = pltpu.VMEM((count, ROWS, LANES), F32)
    half_tile = pltpu.VMEM((count, HALF, LANES), F32)
    flat = (bricks, orients * cells, channels)
    shapes = (target.shape, flat, first_layer.shape, last_layer.shape)
    results = pl.pallas_call(
        functools.partial(step_kernel, along_x, along_y, capacity),
        out_shape=[pltpu.VMEM(shape, F32) for shape in shapes],
        in_specs=[vmem] * 8,
        out_specs=[vmem] * 4,
        scratch_shapes=[
            pltpu.VMEM((ROWS, total), F32),
            pltpu.VMEM((ROWS, rays), F32),
            pltpu.VMEM((bricks, ROWS, units), F32),
            tile, tile, half_tile, half_tile, half_tile, half_tile,
            pltpu.VMEM((bricks, channels, orients * cells), BF16),
            pltpu.VMEM((bricks, units, channels), BF16),
            pltpu.VMEM((bricks, orients * cells, slots), BF16),
            pltpu.VMEM((bricks, channels, slots), BF16),
            pltpu.VMEM((bricks, units, slots), BF16),
            pltpu.VMEM((bricks, ROWS, slots), F32),
            pltpu.VMEM((bricks, ROWS, units), F32),
            pltpu.SemaphoreType.DMA((3, count)),
            pltpu.SemaphoreType.DMA((3, count)),
        ],
        compiler_params=pltpu.CompilerParams(
            collective_id=0, has_side_effects=True, vmem_limit_bytes=48 * 1024 * 1024
        ),
    )(brick_ids.T, cell_index, cell_frac, step_length, target, planes, first_layer, last_layer)
    colour, plane_grad, first_grad, last_grad = pl.pallas_call(
        hand_out,
        out_shape=[jax.ShapeDtypeStruct(shape, F32) for shape in shapes],
        in_specs=[vmem] * 4,
        out_specs=[pl.BlockSpec(memory_space=pl.ANY)] * 4,
        scratch_shapes=[pltpu.SemaphoreType.DMA((4,))],
    )(*results)
    return colour, plane_grad.reshape(planes.shape), first_grad, last_grad


def solution(mesh):
    along_x, along_y = mesh.shape["bx"], mesh.shape["by"]
    return jax.shard_map(
        functools.partial(on_device, along_x, along_y),
        mesh=mesh,
        in_specs=(
            P(("bx", "by"), None),
            P(None, None, None, ("bx", "by")),
            P(None, None, None, ("bx", "by")),
            P(None, None, ("bx", "by")),
            P(None, ("bx", "by")),
            P(("bx", "by"), None, None, None),
            P(("bx", "by"), None, None),
            P(("bx", "by"), None, None),
        ),
        out_specs=(
            P(None, ("bx", "by")),
            P(("bx", "by"), None, None, None),
            P(("bx", "by"), None, None),
            P(("bx", "by"), None, None),
        ),
        check_vma=False,
    )
```

```python
import functools

import jax
import jax.numpy as jnp
from jax import lax
from jax.experimental import pallas as pl
from jax.experimental.pallas import tpu as pltpu
from jax.sharding import PartitionSpec as P

MESH = pl.DeviceIdType.MESH
F32 = jnp.float32
BF16 = jnp.bfloat16
LANES = 128
ROWS = 8
CHUNK = 256
HALF = 4


def matmul(lhs, rhs, contract):
    return lax.dot_general(lhs, rhs, (contract, ((), ())), preferred_element_type=F32)


def parts_of(value, number):
    parts = []
    for _ in range(number - 1):
        part = value.astype(BF16).astype(F32)
        parts.append(part)
        value = value - part
    return parts + [value]


def step_kernel(
    along_x, along_y, capacity,
    ids_ref, cell_ref, frac_ref, step_ref, target_ref, last_ref, planes_hbm, first_hbm,
    colour_ref, corner, feature, hidden, raw_cot, first_ref, last_wide,
    payload, target_tile, planes_ref, slope,
    out_a, in_a, out_b, in_b, out_c, in_c,
    planes_t, first_t,
    load_sem, send_sem, recv_sem,
):
    count = along_x * along_y
    bricks, orients, cells, channels = planes_ref.shape
    side = 1
    while side * side < cells:
        side = side * 2
    crossed, samples, rays = step_ref.shape
    points = crossed * samples
    total = points * rays
    segments = crossed * rays
    width = capacity * samples
    slots = corner.shape[2]
    all_bricks = bricks * count
    me = lax.axis_index("bx") * along_y + lax.axis_index("by")

    load_planes = pltpu.make_async_copy(planes_hbm, planes_ref, load_sem.at[0])
    load_first = pltpu.make_async_copy(first_hbm, first_ref, load_sem.at[1])
    load_planes.start()
    load_first.start()

    def device(number):
        return (lax.div(number, along_y), lax.rem(number, along_y))

    def ahead(offset):
        return device(lax.rem(me + offset, count))

    def behind(offset):
        return device(lax.rem(me + count - offset, count))

    def transfer(phase, source, landing, offset, peer):
        return pltpu.make_async_remote_copy(
            src_ref=source.at[offset],
            dst_ref=landing.at[offset],
            send_sem=send_sem.at[phase, offset],
            recv_sem=recv_sem.at[phase, offset],
            device_id=peer,
            device_id_type=MESH,
        )

    barrier = pltpu.get_barrier_semaphore()

    def greet(offset, carry):
        pl.semaphore_signal(barrier, inc=1, device_id=ahead(offset), device_id_type=MESH)
        return carry

    lax.fori_loop(1, count, greet, 0)

    ids = [ids_ref[pl.ds(k, 1), :] for k in range(crossed)]
    ids_row = jnp.concatenate(ids, axis=1)
    member = lax.broadcasted_iota(jnp.int32, (all_bricks, segments), 0) == ids_row
    member_f = jnp.where(member, 1.0, 0.0).astype(F32)
    earlier = lax.broadcasted_iota(jnp.int32, (segments, segments), 0) < lax.broadcasted_iota(
        jnp.int32, (segments, segments), 1
    )
    ranks = matmul(
        member_f.astype(BF16), jnp.where(earlier, 1.0, 0.0).astype(BF16), ((1,), (0,))
    )
    ranking = jnp.sum(member_f * ranks, axis=0, keepdims=True).astype(jnp.int32)
    shift = bricks.bit_length() - 1
    away = lax.shift_right_logical(ids_row, shift) - me
    away = jnp.where(away < 0, away + count, away)
    place = (ids_row & (bricks - 1)) * width + ranking
    away_all, place_all = [], []
    for k in range(crossed):
        block = slice(k * rays, (k + 1) * rays)
        for s in range(samples):
            away_all.append(away[:, block])
            place_all.append(place[:, block] + s * capacity)
    away_all = jnp.concatenate(away_all, axis=1)
    place_all = jnp.concatenate(place_all, axis=1)
    lane_hot = jnp.where(
        lax.broadcasted_iota(jnp.int32, (LANES, total), 0) == place_all, 1.0, 0.0
    ).astype(BF16)
    whole = lax.broadcasted_iota(jnp.int32, (count, ROWS, total), 0) == away_all[None]
    halves_of = (count // 2, ROWS, total)
    paired = (
        2 * lax.broadcasted_iota(jnp.int32, halves_of, 0)
        + lax.shift_right_logical(lax.broadcasted_iota(jnp.int32, halves_of, 1), 2)
    ) == away_all[None]

    def scatter(value, chosen, number):
        tiles = chosen.shape[0]
        height = tiles * ROWS
        spread = jnp.concatenate(
            [
                jnp.where(chosen, part[None], 0.0).reshape(height, total).astype(BF16)
                for part in parts_of(value, number)
            ],
            axis=0,
        )
        placed = matmul(spread, lane_hot, ((1,), (1,)))
        merged = placed[:height]
        for at in range(1, number):
            merged = merged + placed[at * height : (at + 1) * height]
        return merged.reshape(tiles, ROWS, LANES)

    payload[...] = jnp.zeros_like(payload)
    for k in range(crossed):
        for s in range(samples):
            lanes = pl.ds((k * samples + s) * rays, rays)
            for axis in range(2 * orients):
                payload[pl.ds(axis, 1), lanes] = (
                    cell_ref[axis, k, pl.ds(s, 1), :].astype(F32)
                    + frac_ref[axis, k, pl.ds(s, 1), :]
                )
    tiles = scatter(payload[...], whole, 3)
    out_a[...] = tiles
    in_a[0] = tiles[0]

    pl.semaphore_wait(barrier, count - 1)

    def send_a(offset, carry):
        transfer(0, out_a, in_a, offset, ahead(offset)).start()
        return carry

    lax.fori_loop(1, count, send_a, 0)

    load_planes.wait()
    load_first.wait()
    for b in range(bricks):
        for orient in range(orients):
            planes_t[b, :, pl.ds(orient * cells, cells)] = planes_ref[b, orient].T
        first_t[b] = first_ref[b].T
    last_wide[...] = jnp.zeros_like(last_wide)
    for b in range(bricks):
        last_wide[b, pl.ds(0, HALF), :] = last_ref[b].astype(F32)
    target_tile[...] = jnp.zeros_like(target_tile)
    target_tile[pl.ds(1, 3), :] = target_ref[...]
    target_tile[pl.ds(HALF + 1, 3), :] = target_ref[...]

    row = lax.broadcasted_iota(jnp.int32, (ROWS, LANES), 0)
    lane = lax.broadcasted_iota(jnp.int32, (ROWS, LANES), 1)
    lines = lax.broadcasted_iota(jnp.int32, (side, CHUNK), 0).astype(F32)
    chunk_row = lax.broadcasted_iota(jnp.int32, (ROWS, CHUNK), 0)

    def moved(tile, amount):
        return pltpu.roll(tile, amount % LANES, 1) if amount % LANES else tile

    def columns(landing, b, block):
        height = landing.shape[1]
        at = lane[:height]
        value = jnp.zeros((height, LANES), F32)
        base = block * LANES
        for t in range(base // width, min(count - 1, (base + LANES - 1) // width) + 1):
            low = width * t - base
            value = jnp.where(
                (at >= low) & (at < low + width),
                moved(landing[t], width * (t - b)),
                value,
            )
        return value

    def tile_of(blocks, t):
        value = jnp.zeros((ROWS, LANES), F32)
        base = width * t
        for b in range(bricks):
            for block in range(base // LANES, (base + width - 1) // LANES + 1):
                low = max(block * LANES, base) - base + b * width
                high = min((block + 1) * LANES, base + width) - base + b * width
                value = jnp.where(
                    (lane >= low) & (lane < high),
                    moved(blocks[b][block], width * (b - t)),
                    value,
                )
        return value

    def wait_a(offset, carry):
        transfer(0, out_a, in_a, offset, ahead(offset)).wait_recv()
        return carry

    def send_b(offset, carry):
        transfer(1, out_b, in_b, offset, behind(offset)).start()
        return carry

    blocks = [[] for _ in range(bricks)]
    arrived, returned = 1, 0
    for chunk in range(slots // CHUNK):
        stop = (chunk + 1) * CHUNK
        lanes = pl.ds(chunk * CHUNK, CHUNK)
        needed = min(count, (stop - 1) // width + 1)
        if needed > arrived:
            lax.fori_loop(arrived, needed, wait_a, 0)
            arrived = needed
        for b in range(bricks):
            spots = jnp.concatenate(
                [columns(in_a, b, at) for at in range(chunk * CHUNK // LANES, stop // LANES)],
                axis=1,
            )
            for orient in range(orients):
                near_a = jnp.maximum(
                    0.0, 1.0 - jnp.abs(spots[2 * orient : 2 * orient + 1] - lines)
                )
                near_b = jnp.maximum(
                    0.0, 1.0 - jnp.abs(spots[2 * orient + 1 : 2 * orient + 2] - lines)
                )
                weights = near_a[:, None, :] * near_b[None, :, :]
                corner[b, pl.ds(orient * cells, cells), lanes] = weights.reshape(
                    cells, CHUNK
                ).astype(BF16)
            mixed = matmul(planes_t[b], corner[b, :, lanes], ((1,), (0,))).astype(BF16)
            feature[b, :, lanes] = mixed
            before = matmul(first_t[b], mixed, ((1,), (0,)))
            active = jnp.maximum(before, 0.0).astype(BF16)
            hidden[b, :, lanes] = active
            raw = matmul(last_wide[b].astype(BF16), active, ((1,), (0,)))
            gate = jax.nn.sigmoid(raw)
            soft = jnp.maximum(raw, 0.0) + jnp.log1p(jnp.exp(-jnp.abs(raw)))
            answer = jnp.where(chunk_row == 0, soft, gate)
            slope[b, :, lanes] = jnp.where(chunk_row == 0, gate, gate * (1.0 - gate))
            for at in range(CHUNK // LANES):
                blocks[b].append(answer[:, at * LANES : (at + 1) * LANES])
        ready = min(count, stop // width)
        for t in range(returned, ready):
            out_b[t] = tile_of(blocks, t)[:HALF]
        if ready > max(returned, 1):
            lax.fori_loop(max(returned, 1), ready, send_b, 0)
        returned = max(returned, ready)
    in_b[0] = out_b[0]

    def wait_b(offset, carry):
        transfer(1, out_b, in_b, offset, behind(offset)).wait_recv()
        return carry

    lax.fori_loop(1, count, wait_b, 0)

    held = jnp.concatenate([in_b[t] for t in range(count)], axis=0)
    found = matmul(
        jnp.concatenate([part.astype(BF16) for part in parts_of(held, 2)], axis=0),
        lane_hot,
        ((1,), (0,)),
    )
    found = (found[: count * HALF] + found[count * HALF :]).reshape(halves_of)
    found = jnp.sum(jnp.where(paired, found, 0.0), axis=0)
    found = found[:HALF] + found[HALF:]
    found = jnp.concatenate([found, found], axis=0)
    views = [found[:, i * rays : (i + 1) * rays] for i in range(points)]
    lengths = [
        step_ref[k, pl.ds(s, 1), :] for k in range(crossed) for s in range(samples)
    ]
    running = jnp.zeros((1, rays), F32)
    colour = jnp.zeros((ROWS, rays), F32)
    weights, passed = [], []
    for i in range(points):
        depth = views[i][0:1] * lengths[i]
        weight = jnp.exp(-running) * (1.0 - jnp.exp(-depth))
        running = running + depth
        passed.append(jnp.exp(-running))
        weights.append(weight)
        colour = colour + weight * views[i]
    colour_ref[...] = colour[1:4]
    residual = jnp.where((row & 3) > 0, colour - target_tile[...], 0.0)
    behind_sum = jnp.zeros((1, rays), F32)
    cotangents = [None] * points
    for i in reversed(range(points)):
        shade_dot = jnp.sum((views[i] * residual)[:HALF], axis=0, keepdims=True)
        density_cot = (passed[i] * shade_dot - behind_sum) * lengths[i]
        behind_sum = behind_sum + weights[i] * shade_dot
        cotangents[i] = jnp.where((row & 3) == 0, density_cot, weights[i] * residual)
    tiles = scatter(jnp.concatenate(cotangents, axis=1), paired, 2)
    for t in range(count):
        out_c[t] = tiles[t // 2, (t % 2) * HALF : (t % 2 + 1) * HALF]
    in_c[0] = out_c[0]

    def send_c(offset, carry):
        transfer(2, out_c, in_c, offset, ahead(offset)).start()
        return carry

    lax.fori_loop(1, count, send_c, 0)

    def drain(offset, carry):
        transfer(0, out_a, in_a, offset, ahead(offset)).wait_send()
        transfer(1, out_b, in_b, offset, behind(offset)).wait_send()
        transfer(2, out_c, in_c, offset, ahead(offset)).wait()
        return carry

    lax.fori_loop(1, count, drain, 0)
    for b in range(bricks):
        for block in range(slots // LANES):
            lanes = pl.ds(block * LANES, LANES)
            pull = columns(in_c, b, block)
            raw_cot[b, :, lanes] = (
                jnp.concatenate([pull, jnp.zeros_like(pull)], axis=0) * slope[b, :, lanes]
            )


def gradient_kernel(
    colour_in, corner, feature, hidden, raw_cot, first_ref, last_wide,
    colour_out, plane_out, first_out, last_out,
    plane_part, first_part, last_part, before_cot, feature_cot, sems,
):
    bricks, _, slots = corner.shape
    copies = [pltpu.make_async_copy(colour_in, colour_out, sems.at[0])]
    copies[0].start()
    for b in range(bricks):
        cot = raw_cot[b].astype(BF16)
        for chunk in range(slots // CHUNK):
            lanes = pl.ds(chunk * CHUNK, CHUNK)
            pull = matmul(
                last_wide[b].astype(BF16),
                cot[:, chunk * CHUNK : (chunk + 1) * CHUNK],
                ((0,), (0,)),
            )
            masked = jnp.where(hidden[b, :, lanes].astype(F32) > 0.0, pull, 0.0).astype(BF16)
            before_cot[:, lanes] = masked
            feature_cot[:, lanes] = matmul(first_ref[b], masked, ((1,), (0,))).astype(BF16)
        plane_part[b] = matmul(corner[b], feature_cot[...], ((1,), (1,)))
        first_part[b] = matmul(feature[b], before_cot[...], ((1,), (1,)))
        last_part[b] = matmul(cot, hidden[b], ((1,), (1,)))[:HALF]
        for at, (source, landing) in enumerate(
            ((plane_part, plane_out), (first_part, first_out), (last_part, last_out))
        ):
            copy = pltpu.make_async_copy(source.at[b], landing.at[b], sems.at[1 + 3 * b + at])
            copy.start()
            copies.append(copy)
    for copy in copies:
        copy.wait()


def on_device(
    along_x, along_y,
    brick_ids, cell_index, cell_frac, step_length, target, planes, first_layer, last_layer,
):
    count = along_x * along_y
    bricks, orients, cells, channels = planes.shape
    units = first_layer.shape[2]
    rays, crossed = brick_ids.shape
    samples = step_length.shape[1]
    all_bricks = bricks * count
    capacity = max(2, (3 * rays * crossed + all_bricks - 1) // all_bricks)
    width = capacity * samples
    assert bricks == 2 and bricks * width <= LANES and count % 2 == 0
    slots = (count * width + CHUNK - 1) // CHUNK * CHUNK
    total = crossed * samples * rays
    flat = (bricks, orients * cells, channels)
    vmem = pl.BlockSpec(memory_space=pltpu.VMEM)
    hbm = pl.BlockSpec(memory_space=pltpu.HBM)
    tile = pltpu.VMEM((count, ROWS, LANES), F32)
    half_tile = pltpu.VMEM((count, HALF, LANES), F32)
    limit = 32 * 1024 * 1024
    inputs = (
        brick_ids.T, cell_index, cell_frac, step_length, target, last_layer, planes, first_layer
    )
    held = pl.pallas_call(
        functools.partial(step_kernel, along_x, along_y, capacity),
        out_shape=[
            pltpu.VMEM(target.shape, F32),
            pltpu.VMEM((bricks, orients * cells, slots), BF16),
            pltpu.VMEM((bricks, channels, slots), BF16),
            pltpu.VMEM((bricks, units, slots), BF16),
            pltpu.VMEM((bricks, ROWS, slots), F32),
            pltpu.VMEM(first_layer.shape, BF16),
            pltpu.VMEM((bricks, ROWS, units), F32),
        ],
        in_specs=[vmem] * 6 + [hbm] * 2,
        out_specs=[vmem] * 7,
        scratch_shapes=[
            pltpu.VMEM((ROWS, total), F32),
            pltpu.VMEM((ROWS, rays), F32),
            pltpu.VMEM(planes.shape, BF16),
            pltpu.VMEM((bricks, ROWS, slots), F32),
            tile, tile, half_tile, half_tile, half_tile, half_tile,
            pltpu.VMEM((bricks, channels, orients * cells), BF16),
            pltpu.VMEM((bricks, units, channels), BF16),
            pltpu.SemaphoreType.DMA((2,)),
            pltpu.SemaphoreType.DMA((3, count)),
            pltpu.SemaphoreType.DMA((3, count)),
        ],
        compiler_params=pltpu.CompilerParams(
            collective_id=0, has_side_effects=True, vmem_limit_bytes=limit
        ),
    )(*[pltpu.with_memory_space_constraint(value, pltpu.HBM) for value in inputs])
    colour, plane_grad, first_grad, last_grad = pl.pallas_call(
        gradient_kernel,
        out_shape=[
            jax.ShapeDtypeStruct(shape, F32)
            for shape in (target.shape, flat, first_layer.shape, last_layer.shape)
        ],
        in_specs=[vmem] * 7,
        out_specs=[hbm] * 4,
        scratch_shapes=[
            pltpu.VMEM(flat, F32),
            pltpu.VMEM(first_layer.shape, F32),
            pltpu.VMEM(last_layer.shape, F32),
            pltpu.VMEM((units, slots), BF16),
            pltpu.VMEM((channels, slots), BF16),
            pltpu.SemaphoreType.DMA((1 + 3 * bricks,)),
        ],
        compiler_params=pltpu.CompilerParams(vmem_limit_bytes=limit),
    )(*[pltpu.with_memory_space_constraint(value, pltpu.VMEM) for value in held])
    return colour, plane_grad.reshape(planes.shape), first_grad, last_grad


def solution(mesh):
    along_x, along_y = mesh.shape["bx"], mesh.shape["by"]
    return jax.shard_map(
        functools.partial(on_device, along_x, along_y),
        mesh=mesh,
        in_specs=(
            P(("bx", "by"), None),
            P(None, None, None, ("bx", "by")),
            P(None, None, None, ("bx", "by")),
            P(None, None, ("bx", "by")),
            P(None, ("bx", "by")),
            P(("bx", "by"), None, None, None),
            P(("bx", "by"), None, None),
            P(("bx", "by"), None, None),
        ),
        out_specs=(
            P(None, ("bx", "by")),
            P(("bx", "by"), None, None, None),
            P(("bx", "by"), None, None),
            P(("bx", "by"), None, None),
        ),
        check_vma=False,
    )
```

```python
import functools

import jax
import jax.numpy as jnp
from jax import lax
from jax.experimental import pallas as pl
from jax.experimental.pallas import tpu as pltpu
from jax.sharding import PartitionSpec as P

MESH = pl.DeviceIdType.MESH
F32 = jnp.float32
BF16 = jnp.bfloat16
LANES = 128
ROWS = 8
CHUNK = 256
HALF = 4


def matmul(lhs, rhs, contract):
    return lax.dot_general(lhs, rhs, (contract, ((), ())), preferred_element_type=F32)


def parts_of(value, number):
    parts = []
    for _ in range(number - 1):
        part = value.astype(BF16).astype(F32)
        parts.append(part)
        value = value - part
    return parts + [value]


def step_kernel(
    along_x, along_y, capacity,
    ids_ref, cell_ref, frac_ref, step_ref, target_ref, last_ref, planes_hbm, first_hbm,
    colour_ref, corner, feature, hidden, raw_cot, first_ref, last_wide,
    payload, target_tile, planes_ref, spots, answers, slope,
    out_a, in_a, out_b, in_b, out_c, in_c,
    planes_t, first_t,
    load_sem, send_sem, recv_sem,
):
    count = along_x * along_y
    bricks, orients, cells, channels = planes_ref.shape
    side = 1
    while side * side < cells:
        side = side * 2
    crossed, samples, rays = step_ref.shape
    points = crossed * samples
    total = points * rays
    segments = crossed * rays
    width = capacity * samples
    slots = corner.shape[2]
    all_bricks = bricks * count
    me = lax.axis_index("bx") * along_y + lax.axis_index("by")

    load_planes = pltpu.make_async_copy(planes_hbm, planes_ref, load_sem.at[0])
    load_first = pltpu.make_async_copy(first_hbm, first_ref, load_sem.at[1])
    load_planes.start()
    load_first.start()

    shift_y = along_y.bit_length() - 1

    def device(number):
        number = number & (count - 1)
        return (lax.shift_right_logical(number, shift_y), number & (along_y - 1))

    def ahead(offset):
        return device(me + offset)

    def behind(offset):
        return device(me + count - offset)

    def transfer(phase, part, source, landing, where, peer):
        return pltpu.make_async_remote_copy(
            src_ref=source.at[where],
            dst_ref=landing.at[where],
            send_sem=send_sem.at[phase],
            recv_sem=recv_sem.at[phase, part],
            device_id=peer,
            device_id_type=MESH,
        )

    def spread_out(phase, part, source, landing, peer, start, stop):
        def send(offset, carry):
            transfer(phase, part, source, landing, offset, peer(offset)).start()
            return carry

        lax.fori_loop(start, stop, send, 0)

    def gather_in(phase, part, source, landing, start, stop):
        rows = pl.ds(start, stop - start)
        transfer(phase, part, source, landing, rows, ahead(1)).wait_recv()

    def sent(phase, source, landing):
        transfer(phase, 0, source, landing, pl.ds(1, count - 1), ahead(1)).wait_send()

    barrier = pltpu.get_barrier_semaphore()

    def greet(offset, carry):
        pl.semaphore_signal(barrier, inc=1, device_id=ahead(offset), device_id_type=MESH)
        return carry

    lax.fori_loop(1, count, greet, 0)

    ids = [ids_ref[pl.ds(k, 1), :] for k in range(crossed)]
    ids_row = jnp.concatenate(ids, axis=1)
    member = lax.broadcasted_iota(jnp.int32, (all_bricks, segments), 0) == ids_row
    member_f = jnp.where(member, 1.0, 0.0).astype(F32)
    earlier = lax.broadcasted_iota(jnp.int32, (segments, segments), 0) < lax.broadcasted_iota(
        jnp.int32, (segments, segments), 1
    )
    ranks = matmul(
        member_f.astype(BF16), jnp.where(earlier, 1.0, 0.0).astype(BF16), ((1,), (0,))
    )
    ranking = jnp.sum(member_f * ranks, axis=0, keepdims=True).astype(jnp.int32)
    shift = bricks.bit_length() - 1
    away = lax.shift_right_logical(ids_row, shift) - me
    away = jnp.where(away < 0, away + count, away)
    place = (ids_row & (bricks - 1)) * width + ranking
    away_all, place_all = [], []
    for k in range(crossed):
        block = slice(k * rays, (k + 1) * rays)
        for s in range(samples):
            away_all.append(away[:, block])
            place_all.append(place[:, block] + s * capacity)
    away_all = jnp.concatenate(away_all, axis=1)
    place_all = jnp.concatenate(place_all, axis=1)
    lane_hot = jnp.where(
        lax.broadcasted_iota(jnp.int32, (LANES, total), 0) == place_all, 1.0, 0.0
    ).astype(BF16)
    whole = lax.broadcasted_iota(jnp.int32, (count, ROWS, total), 0) == away_all[None]
    halves_of = (count // 2, ROWS, total)
    paired = (
        2 * lax.broadcasted_iota(jnp.int32, halves_of, 0)
        + lax.shift_right_logical(lax.broadcasted_iota(jnp.int32, halves_of, 1), 2)
    ) == away_all[None]

    def scatter(value, chosen, number):
        tiles = chosen.shape[0]
        height = tiles * ROWS
        spread = jnp.concatenate(
            [
                jnp.where(chosen, part[None], 0.0).reshape(height, total).astype(BF16)
                for part in parts_of(value, number)
            ],
            axis=0,
        )
        placed = matmul(spread, lane_hot, ((1,), (1,)))
        merged = placed[:height]
        for at in range(1, number):
            merged = merged + placed[at * height : (at + 1) * height]
        return merged.reshape(tiles, ROWS, LANES)

    payload[...] = jnp.zeros_like(payload)
    for k in range(crossed):
        for s in range(samples):
            lanes = pl.ds((k * samples + s) * rays, rays)
            for axis in range(2 * orients):
                payload[pl.ds(axis, 1), lanes] = (
                    cell_ref[axis, k, pl.ds(s, 1), :].astype(F32)
                    + frac_ref[axis, k, pl.ds(s, 1), :]
                )
    tiles = scatter(payload[...], whole, 3)
    out_a[...] = tiles[:, : 2 * orients]
    in_a[0] = tiles[0, : 2 * orients]

    pl.semaphore_wait(barrier, count - 1)

    chunks = slots // CHUNK
    edges = [0, chunks // 2 * CHUNK, slots]
    reach = [1] + [min(count, (stop - 1) // width + 1) for stop in edges[1:]]
    for part in range(2):
        spread_out(0, part, out_a, in_a, ahead, reach[part], reach[part + 1])

    load_planes.wait()
    load_first.wait()
    for b in range(bricks):
        for orient in range(orients):
            planes_t[b, :, pl.ds(orient * cells, cells)] = planes_ref[b, orient].T
        first_t[b] = first_ref[b].T
    last_wide[...] = jnp.zeros_like(last_wide)
    for b in range(bricks):
        last_wide[b, pl.ds(0, HALF), :] = last_ref[b].astype(F32)
    target_tile[...] = jnp.zeros_like(target_tile)
    target_tile[pl.ds(1, 3), :] = target_ref[...]
    target_tile[pl.ds(HALF + 1, 3), :] = target_ref[...]

    row = lax.broadcasted_iota(jnp.int32, (ROWS, LANES), 0)
    lane = lax.broadcasted_iota(jnp.int32, (ROWS, LANES), 1)
    lines = lax.broadcasted_iota(jnp.int32, (side, CHUNK), 0).astype(F32)
    chunk_row = lax.broadcasted_iota(jnp.int32, (ROWS, CHUNK), 0)

    def moved(tile, amount):
        return pltpu.roll(tile, amount % LANES, 1) if amount % LANES else tile

    def columns(landing, b, block):
        height = landing.shape[1]
        at = lane[:height]
        value = jnp.zeros((height, LANES), F32)
        base = block * LANES
        for t in range(base // width, min(count - 1, (base + LANES - 1) // width) + 1):
            low = width * t - base
            value = jnp.where(
                (at >= low) & (at < low + width),
                moved(landing[t], width * (t - b)),
                value,
            )
        return value

    def tile_of(values, t):
        value = jnp.zeros((ROWS, LANES), F32)
        base = width * t
        for b in range(bricks):
            for block in range(base // LANES, (base + width - 1) // LANES + 1):
                low = max(block * LANES, base) - base + b * width
                high = min((block + 1) * LANES, base + width) - base + b * width
                value = jnp.where(
                    (lane >= low) & (lane < high),
                    moved(values[b, :, pl.ds(block * LANES, LANES)], width * (b - t)),
                    value,
                )
        return value

    def forward(chunk, carry):
        lanes = pl.ds(pl.multiple_of(chunk * CHUNK, CHUNK), CHUNK)
        for b in range(bricks):
            for orient in range(orients):
                near_a = jnp.maximum(
                    0.0, 1.0 - jnp.abs(spots[b, pl.ds(2 * orient, 1), lanes] - lines)
                )
                near_b = jnp.maximum(
                    0.0, 1.0 - jnp.abs(spots[b, pl.ds(2 * orient + 1, 1), lanes] - lines)
                )
                weights = near_a[:, None, :] * near_b[None, :, :]
                corner[b, pl.ds(orient * cells, cells), lanes] = weights.reshape(
                    cells, CHUNK
                ).astype(BF16)
            mixed = matmul(planes_t[b], corner[b, :, lanes], ((1,), (0,))).astype(BF16)
            feature[b, :, lanes] = mixed
            before = matmul(first_t[b], mixed, ((1,), (0,)))
            active = jnp.maximum(before, 0.0).astype(BF16)
            hidden[b, :, lanes] = active
            raw = matmul(last_wide[b].astype(BF16), active, ((1,), (0,)))
            gate = jax.nn.sigmoid(raw)
            soft = jnp.maximum(raw, 0.0) + jnp.log1p(jnp.exp(-jnp.abs(raw)))
            answers[b, :, lanes] = jnp.where(chunk_row == 0, soft, gate)
            slope[b, :, lanes] = jnp.where(chunk_row == 0, gate, gate * (1.0 - gate))
        return carry

    returned = 0
    for part in range(2):
        gather_in(0, part, out_a, in_a, reach[part], reach[part + 1])
        for b in range(bricks):
            for block in range(edges[part] // LANES, edges[part + 1] // LANES):
                spots[b, pl.ds(0, 2 * orients), pl.ds(block * LANES, LANES)] = columns(
                    in_a, b, block
                )
        lax.fori_loop(edges[part] // CHUNK, edges[part + 1] // CHUNK, forward, 0)
        ready = min(count, edges[part + 1] // width)
        for t in range(returned, ready):
            out_b[t] = tile_of(answers, t)[:HALF]
        spread_out(1, 0, out_b, in_b, behind, max(returned, 1), ready)
        returned = ready
    in_b[0] = out_b[0]
    sent(0, out_a, in_a)
    gather_in(1, 0, out_b, in_b, 1, count)

    held = jnp.concatenate([in_b[t] for t in range(count)], axis=0)
    found = matmul(
        jnp.concatenate([part.astype(BF16) for part in parts_of(held, 2)], axis=0),
        lane_hot,
        ((1,), (0,)),
    )
    found = (found[: count * HALF] + found[count * HALF :]).reshape(halves_of)
    found = jnp.sum(jnp.where(paired, found, 0.0), axis=0)
    found = found[:HALF] + found[HALF:]
    found = jnp.concatenate([found, found], axis=0)
    views = [found[:, i * rays : (i + 1) * rays] for i in range(points)]
    lengths = [
        step_ref[k, pl.ds(s, 1), :] for k in range(crossed) for s in range(samples)
    ]
    running = jnp.zeros((1, rays), F32)
    colour = jnp.zeros((ROWS, rays), F32)
    weights, passed = [], []
    for i in range(points):
        depth = views[i][0:1] * lengths[i]
        weight = jnp.exp(-running) * (1.0 - jnp.exp(-depth))
        running = running + depth
        passed.append(jnp.exp(-running))
        weights.append(weight)
        colour = colour + weight * views[i]
    colour_ref[...] = colour[1:4]
    residual = jnp.where((row & 3) > 0, colour - target_tile[...], 0.0)
    behind_sum = jnp.zeros((1, rays), F32)
    cotangents = [None] * points
    for i in reversed(range(points)):
        shade_dot = jnp.sum((views[i] * residual)[:HALF], axis=0, keepdims=True)
        density_cot = (passed[i] * shade_dot - behind_sum) * lengths[i]
        behind_sum = behind_sum + weights[i] * shade_dot
        cotangents[i] = jnp.where((row & 3) == 0, density_cot, weights[i] * residual)
    tiles = scatter(jnp.concatenate(cotangents, axis=1), paired, 2)
    for t in range(count):
        out_c[t] = tiles[t // 2, (t % 2) * HALF : (t % 2 + 1) * HALF]
    in_c[0] = out_c[0]

    def send_c(turn, carry):
        offset = turn + count // 2 - 1
        offset = jnp.where(offset >= count, offset - (count - 1), offset)
        transfer(2, 0, out_c, in_c, offset, ahead(offset)).start()
        return carry

    lax.fori_loop(1, count, send_c, 0)
    sent(1, out_b, in_b)
    gather_in(2, 0, out_c, in_c, 1, count)
    sent(2, out_c, in_c)
    for b in range(bricks):
        for block in range(slots // LANES):
            lanes = pl.ds(block * LANES, LANES)
            pull = columns(in_c, b, block)
            raw_cot[b, :, lanes] = (
                jnp.concatenate([pull, jnp.zeros_like(pull)], axis=0) * slope[b, :, lanes]
            )


def gradient_kernel(
    colour_in, corner, feature, hidden, raw_cot, first_ref, last_wide,
    colour_out, plane_out, first_out, last_out,
    plane_part, first_part, last_part, before_cot, feature_cot, sems,
):
    bricks, _, slots = corner.shape
    colour_copy = pltpu.make_async_copy(colour_in, colour_out, sems.at[0, 3])
    colour_copy.start()

    def result_copies(b):
        pairs = ((plane_part, plane_out), (first_part, first_out), (last_part, last_out))
        return [
            pltpu.make_async_copy(source.at[b], landing.at[b], sems.at[b, at])
            for at, (source, landing) in enumerate(pairs)
        ]

    def one_brick(b, carry):
        cot = raw_cot[b].astype(BF16)
        for chunk in range(slots // CHUNK):
            lanes = pl.ds(chunk * CHUNK, CHUNK)
            pull = matmul(
                last_wide[b].astype(BF16),
                cot[:, chunk * CHUNK : (chunk + 1) * CHUNK],
                ((0,), (0,)),
            )
            masked = jnp.where(hidden[b, :, lanes].astype(F32) > 0.0, pull, 0.0).astype(BF16)
            before_cot[:, lanes] = masked
            feature_cot[:, lanes] = matmul(first_ref[b], masked, ((1,), (0,))).astype(BF16)
        plane_part[b] = matmul(corner[b], feature_cot[...], ((1,), (1,)))
        first_part[b] = matmul(feature[b], before_cot[...], ((1,), (1,)))
        last_part[b] = matmul(cot, hidden[b], ((1,), (1,)))[:HALF]
        for copy in result_copies(b):
            copy.start()
        return carry

    lax.fori_loop(0, bricks, one_brick, 0)
    colour_copy.wait()
    for b in range(bricks):
        for copy in result_copies(b):
            copy.wait()


def on_device(
    along_x, along_y,
    brick_ids, cell_index, cell_frac, step_length, target, planes, first_layer, last_layer,
):
    count = along_x * along_y
    bricks, orients, cells, channels = planes.shape
    units = first_layer.shape[2]
    rays, crossed = brick_ids.shape
    samples = step_length.shape[1]
    all_bricks = bricks * count
    capacity = max(2, (3 * rays * crossed + all_bricks - 1) // all_bricks)
    width = capacity * samples
    assert bricks == 2 and bricks * width <= LANES
    assert count & (count - 1) == 0 and along_y & (along_y - 1) == 0
    slots = (count * width + CHUNK - 1) // CHUNK * CHUNK
    total = crossed * samples * rays
    flat = (bricks, orients * cells, channels)
    vmem = pl.BlockSpec(memory_space=pltpu.VMEM)
    hbm = pl.BlockSpec(memory_space=pltpu.HBM)
    wide = pltpu.VMEM((bricks, ROWS, slots), F32)
    tile = pltpu.VMEM((count, 2 * orients, LANES), F32)
    half_tile = pltpu.VMEM((count, HALF, LANES), F32)
    limit = 32 * 1024 * 1024
    inputs = (
        brick_ids.T, cell_index, cell_frac, step_length, target, last_layer, planes, first_layer
    )
    held = pl.pallas_call(
        functools.partial(step_kernel, along_x, along_y, capacity),
        out_shape=[
            pltpu.VMEM(target.shape, F32),
            pltpu.VMEM((bricks, orients * cells, slots), BF16),
            pltpu.VMEM((bricks, channels, slots), BF16),
            pltpu.VMEM((bricks, units, slots), BF16),
            pltpu.VMEM((bricks, ROWS, slots), F32),
            pltpu.VMEM(first_layer.shape, BF16),
            pltpu.VMEM((bricks, ROWS, units), F32),
        ],
        in_specs=[vmem] * 6 + [hbm] * 2,
        out_specs=[vmem] * 7,
        scratch_shapes=[
            pltpu.VMEM((ROWS, total), F32),
            pltpu.VMEM((ROWS, rays), F32),
            pltpu.VMEM(planes.shape, BF16),
            wide, wide, wide,
            tile, tile, half_tile, half_tile, half_tile, half_tile,
            pltpu.VMEM((bricks, channels, orients * cells), BF16),
            pltpu.VMEM((bricks, units, channels), BF16),
            pltpu.SemaphoreType.DMA((2,)),
            pltpu.SemaphoreType.DMA((3,)),
            pltpu.SemaphoreType.DMA((3, 2)),
        ],
        compiler_params=pltpu.CompilerParams(
            collective_id=0, has_side_effects=True, vmem_limit_bytes=limit
        ),
    )(*[pltpu.with_memory_space_constraint(value, pltpu.HBM) for value in inputs])
    colour, plane_grad, first_grad, last_grad = pl.pallas_call(
        gradient_kernel,
        out_shape=[
            jax.ShapeDtypeStruct(shape, F32)
            for shape in (target.shape, flat, first_layer.shape, last_layer.shape)
        ],
        in_specs=[vmem] * 7,
        out_specs=[hbm] * 4,
        scratch_shapes=[
            pltpu.VMEM(flat, F32),
            pltpu.VMEM(first_layer.shape, F32),
            pltpu.VMEM(last_layer.shape, F32),
            pltpu.VMEM((units, slots), BF16),
            pltpu.VMEM((channels, slots), BF16),
            pltpu.SemaphoreType.DMA((bricks, 4)),
        ],
        compiler_params=pltpu.CompilerParams(vmem_limit_bytes=limit),
    )(*[pltpu.with_memory_space_constraint(value, pltpu.VMEM) for value in held])
    return colour, plane_grad.reshape(planes.shape), first_grad, last_grad


def solution(mesh):
    along_x, along_y = mesh.shape["bx"], mesh.shape["by"]
    return jax.shard_map(
        functools.partial(on_device, along_x, along_y),
        mesh=mesh,
        in_specs=(
            P(("bx", "by"), None),
            P(None, None, None, ("bx", "by")),
            P(None, None, None, ("bx", "by")),
            P(None, None, ("bx", "by")),
            P(None, ("bx", "by")),
            P(("bx", "by"), None, None, None),
            P(("bx", "by"), None, None),
            P(("bx", "by"), None, None),
        ),
        out_specs=(
            P(None, ("bx", "by")),
            P(("bx", "by"), None, None, None),
            P(("bx", "by"), None, None),
            P(("bx", "by"), None, None),
        ),
        check_vma=False,
    )
```

```python
import functools

import jax
import jax.numpy as jnp
from jax import lax
from jax.experimental import pallas as pl
from jax.experimental.pallas import tpu as pltpu
from jax.sharding import PartitionSpec as P

MESH = pl.DeviceIdType.MESH
F32 = jnp.float32
BF16 = jnp.bfloat16
LANES = 128
ROWS = 8
CHUNK = 256
HALF = 4


def matmul(lhs, rhs, contract):
    return lax.dot_general(lhs, rhs, (contract, ((), ())), preferred_element_type=F32)


def parts_of(value, number):
    parts = []
    for _ in range(number - 1):
        part = value.astype(BF16).astype(F32)
        parts.append(part)
        value = value - part
    return parts + [value]


def step_kernel(
    along_x, along_y, capacity,
    ids_ref, cell_ref, frac_ref, step_ref, target_ref, last_ref, planes_hbm, first_hbm,
    colour_ref, corner, feature, hidden, raw_cot, first_ref, last_wide,
    payload, target_tile, planes_ref, spots, answers, slope,
    out_a, in_a, out_b, in_b, out_c, in_c,
    planes_t, first_t,
    load_sem, send_sem, recv_sem,
):
    count = along_x * along_y
    bricks, orients, cells, channels = planes_ref.shape
    side = 1
    while side * side < cells:
        side = side * 2
    crossed, samples, rays = step_ref.shape
    points = crossed * samples
    total = points * rays
    segments = crossed * rays
    width = capacity * samples
    slots = corner.shape[2]
    all_bricks = bricks * count
    me = lax.axis_index("bx") * along_y + lax.axis_index("by")

    load_planes = pltpu.make_async_copy(planes_hbm, planes_ref, load_sem.at[0])
    load_first = pltpu.make_async_copy(first_hbm, first_ref, load_sem.at[1])
    load_planes.start()
    load_first.start()

    shift_y = along_y.bit_length() - 1

    def device(number):
        number = number & (count - 1)
        return (lax.shift_right_logical(number, shift_y), number & (along_y - 1))

    def ahead(offset):
        return device(me + offset)

    def behind(offset):
        return device(me + count - offset)

    def transfer(phase, part, source, landing, where, peer):
        return pltpu.make_async_remote_copy(
            src_ref=source.at[where],
            dst_ref=landing.at[where],
            send_sem=send_sem.at[phase],
            recv_sem=recv_sem.at[phase, part],
            device_id=peer,
            device_id_type=MESH,
        )

    def spread_out(phase, part, source, landing, peer, start, stop):
        def send(offset, carry):
            transfer(phase, part, source, landing, offset, peer(offset)).start()
            return carry

        lax.fori_loop(start, stop, send, 0, unroll=True)

    def gather_in(phase, part, source, landing, start, stop):
        rows = pl.ds(start, stop - start)
        transfer(phase, part, source, landing, rows, ahead(1)).wait_recv()

    def sent(phase, source, landing):
        transfer(phase, 0, source, landing, pl.ds(1, count - 1), ahead(1)).wait_send()

    barrier = pltpu.get_barrier_semaphore()

    def greet(offset, carry):
        pl.semaphore_signal(barrier, inc=1, device_id=ahead(offset), device_id_type=MESH)
        return carry

    lax.fori_loop(1, count, greet, 0)

    ids = [ids_ref[pl.ds(k, 1), :] for k in range(crossed)]
    ids_row = jnp.concatenate(ids, axis=1)
    member = lax.broadcasted_iota(jnp.int32, (all_bricks, segments), 0) == ids_row
    member_f = jnp.where(member, 1.0, 0.0).astype(F32)
    earlier = lax.broadcasted_iota(jnp.int32, (segments, segments), 0) < lax.broadcasted_iota(
        jnp.int32, (segments, segments), 1
    )
    ranks = matmul(
        member_f.astype(BF16), jnp.where(earlier, 1.0, 0.0).astype(BF16), ((1,), (0,))
    )
    ranking = jnp.sum(member_f * ranks, axis=0, keepdims=True).astype(jnp.int32)
    shift = bricks.bit_length() - 1
    away = lax.shift_right_logical(ids_row, shift) - me
    away = jnp.where(away < 0, away + count, away)
    place = (ids_row & (bricks - 1)) * width + ranking
    away_all, place_all = [], []
    for k in range(crossed):
        block = slice(k * rays, (k + 1) * rays)
        for s in range(samples):
            away_all.append(away[:, block])
            place_all.append(place[:, block] + s * capacity)
    away_all = jnp.concatenate(away_all, axis=1)
    place_all = jnp.concatenate(place_all, axis=1)
    lane_hot = jnp.where(
        lax.broadcasted_iota(jnp.int32, (LANES, total), 0) == place_all, 1.0, 0.0
    ).astype(BF16)
    def whole(start, stop):
        shape = (stop - start, ROWS, total)
        return lax.broadcasted_iota(jnp.int32, shape, 0) + start == away_all[None]

    def paired(start, stop):
        shape = ((stop - start) // 2, ROWS, total)
        return (
            2 * lax.broadcasted_iota(jnp.int32, shape, 0)
            + lax.shift_right_logical(lax.broadcasted_iota(jnp.int32, shape, 1), 2)
            + start
        ) == away_all[None]

    def scatter(parts, chosen):
        tiles = chosen.shape[0]
        height = tiles * ROWS
        spread = jnp.concatenate(
            [
                jnp.where(chosen, part[None], 0.0).reshape(height, total).astype(BF16)
                for part in parts
            ],
            axis=0,
        )
        placed = matmul(spread, lane_hot, ((1,), (1,)))
        merged = placed[:height]
        for at in range(1, len(parts)):
            merged = merged + placed[at * height : (at + 1) * height]
        return merged.reshape(tiles, ROWS, LANES)

    payload[...] = jnp.zeros_like(payload)
    for k in range(crossed):
        for s in range(samples):
            lanes = pl.ds((k * samples + s) * rays, rays)
            for axis in range(2 * orients):
                payload[pl.ds(axis, 1), lanes] = (
                    cell_ref[axis, k, pl.ds(s, 1), :].astype(F32)
                    + frac_ref[axis, k, pl.ds(s, 1), :]
                )
    edges = [0, slots // 2, slots]
    reach = [1] + [min(count, (stop - 1) // width + 1) for stop in edges[1:]]
    ready = [0, edges[1] // width // 2 * 2, count]
    payload_parts = parts_of(payload[...], 3)
    for part in range(2):
        start, stop = (0, reach[1]) if part == 0 else (reach[1], count)
        tiles = scatter(payload_parts, whole(start, stop))
        out_a[pl.ds(start, stop - start)] = tiles[:, : 2 * orients]
        if part == 0:
            in_a[0] = tiles[0, : 2 * orients]
            pl.semaphore_wait(barrier, count - 1)
        spread_out(0, part, out_a, in_a, ahead, max(start, 1), stop)

    load_planes.wait()
    load_first.wait()
    for b in range(bricks):
        for orient in range(orients):
            planes_t[b, :, pl.ds(orient * cells, cells)] = planes_ref[b, orient].T
        first_t[b] = first_ref[b].T
    last_wide[...] = jnp.zeros_like(last_wide)
    for b in range(bricks):
        last_wide[b, pl.ds(0, HALF), :] = last_ref[b].astype(F32)
    target_tile[...] = jnp.zeros_like(target_tile)
    target_tile[pl.ds(1, 3), :] = target_ref[...]
    target_tile[pl.ds(HALF + 1, 3), :] = target_ref[...]

    row = lax.broadcasted_iota(jnp.int32, (ROWS, LANES), 0)
    lane = lax.broadcasted_iota(jnp.int32, (ROWS, LANES), 1)
    lines = lax.broadcasted_iota(jnp.int32, (side, slots // 2), 0).astype(F32)
    half_row = lax.broadcasted_iota(jnp.int32, (ROWS, slots // 2), 0)

    def moved(tile, amount):
        return pltpu.roll(tile, amount % LANES, 1) if amount % LANES else tile

    def columns(landing, b, block):
        height = landing.shape[1]
        at = lane[:height]
        value = jnp.zeros((height, LANES), F32)
        base = block * LANES
        for t in range(base // width, min(count - 1, (base + LANES - 1) // width) + 1):
            low = width * t - base
            value = jnp.where(
                (at >= low) & (at < low + width),
                moved(landing[t], width * (t - b)),
                value,
            )
        return value

    def tile_of(values, t):
        value = jnp.zeros((ROWS, LANES), F32)
        base = width * t
        for b in range(bricks):
            for block in range(base // LANES, (base + width - 1) // LANES + 1):
                low = max(block * LANES, base) - base + b * width
                high = min((block + 1) * LANES, base + width) - base + b * width
                value = jnp.where(
                    (lane >= low) & (lane < high),
                    moved(values[b, :, pl.ds(block * LANES, LANES)], width * (b - t)),
                    value,
                )
        return value

    def forward(part):
        lanes = pl.ds(edges[part], slots // 2)
        for b in range(bricks):
            for orient in range(orients):
                near_a = jnp.maximum(
                    0.0, 1.0 - jnp.abs(spots[b, pl.ds(2 * orient, 1), lanes] - lines)
                )
                near_b = jnp.maximum(
                    0.0, 1.0 - jnp.abs(spots[b, pl.ds(2 * orient + 1, 1), lanes] - lines)
                )
                weights = near_a[:, None, :] * near_b[None, :, :]
                corner[b, pl.ds(orient * cells, cells), lanes] = weights.reshape(
                    cells, slots // 2
                ).astype(BF16)
            mixed = matmul(planes_t[b], corner[b, :, lanes], ((1,), (0,))).astype(BF16)
            feature[b, :, lanes] = mixed
            before = matmul(first_t[b], mixed, ((1,), (0,)))
            active = jnp.maximum(before, 0.0).astype(BF16)
            hidden[b, :, lanes] = active
            raw = matmul(last_wide[b].astype(BF16), active, ((1,), (0,)))
            gate = jax.nn.sigmoid(raw)
            soft = jnp.maximum(raw, 0.0) + jnp.log1p(jnp.exp(-jnp.abs(raw)))
            answers[b, :, lanes] = jnp.where(half_row == 0, soft, gate)
            slope[b, :, lanes] = jnp.where(half_row == 0, gate, gate * (1.0 - gate))

    for part in range(2):
        gather_in(0, part, out_a, in_a, reach[part], reach[part + 1])
        for b in range(bricks):
            for block in range(edges[part] // LANES, edges[part + 1] // LANES):
                spots[b, pl.ds(0, 2 * orients), pl.ds(block * LANES, LANES)] = columns(
                    in_a, b, block
                )
        forward(part)
        for t in range(ready[part], ready[part + 1]):
            out_b[t] = tile_of(answers, t)[:HALF]
        spread_out(1, part, out_b, in_b, behind, max(ready[part], 1), ready[part + 1])
    in_b[0] = out_b[0]
    sent(0, out_a, in_a)

    found = jnp.zeros((ROWS, total), F32)
    for part in range(2):
        start, stop = ready[part], ready[part + 1]
        gather_in(1, part, out_b, in_b, max(start, 1), stop)
        held = jnp.concatenate([in_b[t] for t in range(start, stop)], axis=0)
        taken = matmul(
            jnp.concatenate([value.astype(BF16) for value in parts_of(held, 2)], axis=0),
            lane_hot,
            ((1,), (0,)),
        )
        height = (stop - start) * HALF
        taken = (taken[:height] + taken[height:]).reshape(height // ROWS, ROWS, total)
        found = found + jnp.sum(jnp.where(paired(start, stop), taken, 0.0), axis=0)
    found = found[:HALF] + found[HALF:]
    found = jnp.concatenate([found, found], axis=0)
    views = [found[:, i * rays : (i + 1) * rays] for i in range(points)]
    lengths = [
        step_ref[k, pl.ds(s, 1), :] for k in range(crossed) for s in range(samples)
    ]
    running = jnp.zeros((1, rays), F32)
    colour = jnp.zeros((ROWS, rays), F32)
    weights, passed = [], []
    for i in range(points):
        depth = views[i][0:1] * lengths[i]
        weight = jnp.exp(-running) * (1.0 - jnp.exp(-depth))
        running = running + depth
        passed.append(jnp.exp(-running))
        weights.append(weight)
        colour = colour + weight * views[i]
    colour_ref[...] = colour[1:4]
    residual = jnp.where((row & 3) > 0, colour - target_tile[...], 0.0)
    behind_sum = jnp.zeros((1, rays), F32)
    cotangents = [None] * points
    for i in reversed(range(points)):
        shade_dot = jnp.sum((views[i] * residual)[:HALF], axis=0, keepdims=True)
        density_cot = (passed[i] * shade_dot - behind_sum) * lengths[i]
        behind_sum = behind_sum + weights[i] * shade_dot
        cotangents[i] = jnp.where((row & 3) == 0, density_cot, weights[i] * residual)
    cotangent_parts = parts_of(jnp.concatenate(cotangents, axis=1), 2)
    middle = count // 2
    for start, stop in ((middle, count), (0, middle)):
        tiles = scatter(cotangent_parts, paired(start, stop))
        for t in range(start, stop):
            at = t - start
            out_c[t] = tiles[at // 2, (at % 2) * HALF : (at % 2 + 1) * HALF]
        spread_out(2, 0, out_c, in_c, ahead, max(start, 1), stop)
    in_c[0] = out_c[0]
    sent(1, out_b, in_b)
    gather_in(2, 0, out_c, in_c, 1, count)
    sent(2, out_c, in_c)
    for b in range(bricks):
        for block in range(slots // LANES):
            lanes = pl.ds(block * LANES, LANES)
            pull = columns(in_c, b, block)
            raw_cot[b, :, lanes] = (
                jnp.concatenate([pull, jnp.zeros_like(pull)], axis=0) * slope[b, :, lanes]
            )


def gradient_kernel(
    colour_in, corner, feature, hidden, raw_cot, first_ref, last_wide,
    colour_out, plane_out, first_out, last_out,
    plane_part, first_part, last_part, before_cot, feature_cot, sems,
):
    bricks, _, slots = corner.shape
    colour_copy = pltpu.make_async_copy(colour_in, colour_out, sems.at[0, 3])
    colour_copy.start()

    def result_copies(b):
        pairs = ((plane_part, plane_out), (first_part, first_out), (last_part, last_out))
        return [
            pltpu.make_async_copy(source.at[b], landing.at[b], sems.at[b, at])
            for at, (source, landing) in enumerate(pairs)
        ]

    def one_brick(b, carry):
        cot = raw_cot[b].astype(BF16)
        for chunk in range(slots // CHUNK):
            lanes = pl.ds(chunk * CHUNK, CHUNK)
            pull = matmul(
                last_wide[b].astype(BF16),
                cot[:, chunk * CHUNK : (chunk + 1) * CHUNK],
                ((0,), (0,)),
            )
            masked = jnp.where(hidden[b, :, lanes].astype(F32) > 0.0, pull, 0.0).astype(BF16)
            before_cot[:, lanes] = masked
            feature_cot[:, lanes] = matmul(first_ref[b], masked, ((1,), (0,))).astype(BF16)
        plane_part[b] = matmul(corner[b], feature_cot[...], ((1,), (1,)))
        first_part[b] = matmul(feature[b], before_cot[...], ((1,), (1,)))
        last_part[b] = matmul(cot, hidden[b], ((1,), (1,)))[:HALF]
        for copy in result_copies(b):
            copy.start()
        return carry

    lax.fori_loop(0, bricks, one_brick, 0)
    colour_copy.wait()
    for b in range(bricks):
        for copy in result_copies(b):
            copy.wait()


def on_device(
    along_x, along_y,
    brick_ids, cell_index, cell_frac, step_length, target, planes, first_layer, last_layer,
):
    count = along_x * along_y
    bricks, orients, cells, channels = planes.shape
    units = first_layer.shape[2]
    rays, crossed = brick_ids.shape
    samples = step_length.shape[1]
    all_bricks = bricks * count
    capacity = max(2, (3 * rays * crossed + all_bricks - 1) // all_bricks)
    width = capacity * samples
    assert bricks == 2 and bricks * width <= LANES
    assert count & (count - 1) == 0 and along_y & (along_y - 1) == 0
    slots = (count * width + CHUNK - 1) // CHUNK * CHUNK
    total = crossed * samples * rays
    flat = (bricks, orients * cells, channels)
    vmem = pl.BlockSpec(memory_space=pltpu.VMEM)
    hbm = pl.BlockSpec(memory_space=pltpu.HBM)
    wide = pltpu.VMEM((bricks, ROWS, slots), F32)
    tile = pltpu.VMEM((count, 2 * orients, LANES), F32)
    half_tile = pltpu.VMEM((count, HALF, LANES), F32)
    limit = 32 * 1024 * 1024
    inputs = (
        brick_ids.T, cell_index, cell_frac, step_length, target, last_layer, planes, first_layer
    )
    held = pl.pallas_call(
        functools.partial(step_kernel, along_x, along_y, capacity),
        out_shape=[
            pltpu.VMEM(target.shape, F32),
            pltpu.VMEM((bricks, orients * cells, slots), BF16),
            pltpu.VMEM((bricks, channels, slots), BF16),
            pltpu.VMEM((bricks, units, slots), BF16),
            pltpu.VMEM((bricks, ROWS, slots), F32),
            pltpu.VMEM(first_layer.shape, BF16),
            pltpu.VMEM((bricks, ROWS, units), F32),
        ],
        in_specs=[vmem] * 6 + [hbm] * 2,
        out_specs=[vmem] * 7,
        scratch_shapes=[
            pltpu.VMEM((ROWS, total), F32),
            pltpu.VMEM((ROWS, rays), F32),
            pltpu.VMEM(planes.shape, BF16),
            wide, wide, wide,
            tile, tile, half_tile, half_tile, half_tile, half_tile,
            pltpu.VMEM((bricks, channels, orients * cells), BF16),
            pltpu.VMEM((bricks, units, channels), BF16),
            pltpu.SemaphoreType.DMA((2,)),
            pltpu.SemaphoreType.DMA((3,)),
            pltpu.SemaphoreType.DMA((3, 2)),
        ],
        compiler_params=pltpu.CompilerParams(
            collective_id=0, has_side_effects=True, vmem_limit_bytes=limit
        ),
    )(*[pltpu.with_memory_space_constraint(value, pltpu.HBM) for value in inputs])
    colour, plane_grad, first_grad, last_grad = pl.pallas_call(
        gradient_kernel,
        out_shape=[
            jax.ShapeDtypeStruct(shape, F32)
            for shape in (target.shape, flat, first_layer.shape, last_layer.shape)
        ],
        in_specs=[vmem] * 7,
        out_specs=[hbm] * 4,
        scratch_shapes=[
            pltpu.VMEM(flat, F32),
            pltpu.VMEM(first_layer.shape, F32),
            pltpu.VMEM(last_layer.shape, F32),
            pltpu.VMEM((units, slots), BF16),
            pltpu.VMEM((channels, slots), BF16),
            pltpu.SemaphoreType.DMA((bricks, 4)),
        ],
        compiler_params=pltpu.CompilerParams(vmem_limit_bytes=limit),
    )(*[pltpu.with_memory_space_constraint(value, pltpu.VMEM) for value in held])
    return colour, plane_grad.reshape(planes.shape), first_grad, last_grad


def solution(mesh):
    along_x, along_y = mesh.shape["bx"], mesh.shape["by"]
    return jax.shard_map(
        functools.partial(on_device, along_x, along_y),
        mesh=mesh,
        in_specs=(
            P(("bx", "by"), None),
            P(None, None, None, ("bx", "by")),
            P(None, None, None, ("bx", "by")),
            P(None, None, ("bx", "by")),
            P(None, ("bx", "by")),
            P(("bx", "by"), None, None, None),
            P(("bx", "by"), None, None),
            P(("bx", "by"), None, None),
        ),
        out_specs=(
            P(None, ("bx", "by")),
            P(("bx", "by"), None, None, None),
            P(("bx", "by"), None, None),
            P(("bx", "by"), None, None),
        ),
        check_vma=False,
    )
```

```python
import functools

import jax
import jax.numpy as jnp
from jax import lax
from jax.experimental import pallas as pl
from jax.experimental.pallas import tpu as pltpu
from jax.sharding import PartitionSpec as P

MESH = pl.DeviceIdType.MESH
F32 = jnp.float32
BF16 = jnp.bfloat16
LANES = 128
ROWS = 8
CHUNK = 256
HALF = 4


def matmul(lhs, rhs, contract):
    return lax.dot_general(lhs, rhs, (contract, ((), ())), preferred_element_type=F32)


def parts_of(value, number):
    parts = []
    for _ in range(number - 1):
        part = value.astype(BF16).astype(F32)
        parts.append(part)
        value = value - part
    return parts + [value]


def column_edges(slots):
    first = (slots // 2 + CHUNK - 1) // CHUNK * CHUNK
    return [0, first, slots]


def step_kernel(
    along_x, along_y, capacity,
    ids_ref, cell_ref, frac_ref, step_ref, target_ref, last_ref, planes_hbm, first_hbm,
    colour_ref, corner, feature, hidden, raw_cot, first_ref, last_wide,
    payload, target_tile, planes_ref, spots, answers, slope,
    out_a, in_a, out_b, in_b, out_c, in_c,
    planes_t, first_t,
    load_sem, send_sem, recv_sem,
):
    count = along_x * along_y
    bricks, orients, cells, channels = planes_ref.shape
    side = 1
    while side * side < cells:
        side = side * 2
    crossed, samples, rays = step_ref.shape
    points = crossed * samples
    total = points * rays
    segments = crossed * rays
    width = capacity * samples
    slots = corner.shape[2]
    all_bricks = bricks * count
    me = lax.axis_index("bx") * along_y + lax.axis_index("by")

    load_planes = pltpu.make_async_copy(planes_hbm, planes_ref, load_sem.at[0])
    load_first = pltpu.make_async_copy(first_hbm, first_ref, load_sem.at[1])
    load_planes.start()
    load_first.start()

    shift_y = along_y.bit_length() - 1

    def device(number):
        number = number & (count - 1)
        return (lax.shift_right_logical(number, shift_y), number & (along_y - 1))

    def ahead(offset):
        return device(me + offset)

    def behind(offset):
        return device(me + count - offset)

    def transfer(phase, part, source, landing, where, peer):
        return pltpu.make_async_remote_copy(
            src_ref=source.at[where],
            dst_ref=landing.at[where],
            send_sem=send_sem.at[phase],
            recv_sem=recv_sem.at[phase, part],
            device_id=peer,
            device_id_type=MESH,
        )

    def spread_out(phase, part, source, landing, peer, start, stop):
        def send(offset, carry):
            transfer(phase, part, source, landing, offset, peer(offset)).start()
            return carry

        lax.fori_loop(start, stop, send, 0, unroll=True)

    def gather_in(phase, part, source, landing, start, stop):
        rows = pl.ds(start, stop - start)
        transfer(phase, part, source, landing, rows, ahead(1)).wait_recv()

    def sent(phase, source, landing):
        transfer(phase, 0, source, landing, pl.ds(1, count - 1), ahead(1)).wait_send()

    barrier = pltpu.get_barrier_semaphore()

    def greet(offset, carry):
        pl.semaphore_signal(barrier, inc=1, device_id=ahead(offset), device_id_type=MESH)
        return carry

    lax.fori_loop(1, count, greet, 0)

    ids = [ids_ref[pl.ds(k, 1), :] for k in range(crossed)]
    ids_row = jnp.concatenate(ids, axis=1)
    member = lax.broadcasted_iota(jnp.int32, (all_bricks, segments), 0) == ids_row
    member_f = jnp.where(member, 1.0, 0.0).astype(F32)
    earlier = lax.broadcasted_iota(jnp.int32, (segments, segments), 0) < lax.broadcasted_iota(
        jnp.int32, (segments, segments), 1
    )
    ranks = matmul(
        member_f.astype(BF16), jnp.where(earlier, 1.0, 0.0).astype(BF16), ((1,), (0,))
    )
    ranking = jnp.sum(member_f * ranks, axis=0, keepdims=True).astype(jnp.int32)
    shift = bricks.bit_length() - 1
    away = lax.shift_right_logical(ids_row, shift) - me
    away = jnp.where(away < 0, away + count, away)
    place = (ids_row & (bricks - 1)) * width + ranking
    away_all, place_all = [], []
    for k in range(crossed):
        block = slice(k * rays, (k + 1) * rays)
        for s in range(samples):
            away_all.append(away[:, block])
            place_all.append(place[:, block] + s * capacity)
    away_all = jnp.concatenate(away_all, axis=1)
    place_all = jnp.concatenate(place_all, axis=1)
    lane_hot = jnp.where(
        lax.broadcasted_iota(jnp.int32, (LANES, total), 0) == place_all, 1.0, 0.0
    ).astype(BF16)
    def whole(start, stop):
        shape = (stop - start, ROWS, total)
        return lax.broadcasted_iota(jnp.int32, shape, 0) + start == away_all[None]

    def paired(start, stop):
        shape = ((stop - start) // 2, ROWS, total)
        return (
            2 * lax.broadcasted_iota(jnp.int32, shape, 0)
            + lax.shift_right_logical(lax.broadcasted_iota(jnp.int32, shape, 1), 2)
            + start
        ) == away_all[None]

    def scatter(parts, chosen):
        tiles = chosen.shape[0]
        height = tiles * ROWS
        spread = jnp.concatenate(
            [
                jnp.where(chosen, part[None], 0.0).reshape(height, total).astype(BF16)
                for part in parts
            ],
            axis=0,
        )
        placed = matmul(spread, lane_hot, ((1,), (1,)))
        merged = placed[:height]
        for at in range(1, len(parts)):
            merged = merged + placed[at * height : (at + 1) * height]
        return merged.reshape(tiles, ROWS, LANES)

    payload[...] = jnp.zeros_like(payload)
    for k in range(crossed):
        for s in range(samples):
            lanes = pl.ds((k * samples + s) * rays, rays)
            for axis in range(2 * orients):
                payload[pl.ds(axis, 1), lanes] = (
                    cell_ref[axis, k, pl.ds(s, 1), :].astype(F32)
                    + frac_ref[axis, k, pl.ds(s, 1), :]
                )
    edges = column_edges(slots)
    reach = [1] + [min(count, (stop - 1) // width + 1) for stop in edges[1:]]
    ready = [0, edges[1] // width // 4 * 4, count]
    payload_parts = parts_of(payload[...], 3)
    for part in range(2):
        start, stop = (0, reach[1]) if part == 0 else (reach[1], count)
        tiles = scatter(payload_parts, whole(start, stop))
        out_a[pl.ds(start, stop - start)] = tiles[:, : 2 * orients]
        if part == 0:
            in_a[0] = tiles[0, : 2 * orients]
            pl.semaphore_wait(barrier, count - 1)
        spread_out(0, part, out_a, in_a, ahead, max(start, 1), stop)

    load_planes.wait()
    load_first.wait()
    for b in range(bricks):
        for orient in range(orients):
            planes_t[b, :, pl.ds(orient * cells, cells)] = planes_ref[b, orient].T
        first_t[b] = first_ref[b].T
    last_wide[...] = jnp.zeros_like(last_wide)
    for b in range(bricks):
        last_wide[b, pl.ds(0, HALF), :] = last_ref[b].astype(F32)
    target_tile[...] = jnp.zeros_like(target_tile)
    target_tile[pl.ds(1, 3), :] = target_ref[...]
    target_tile[pl.ds(HALF + 1, 3), :] = target_ref[...]

    row = lax.broadcasted_iota(jnp.int32, (ROWS, LANES), 0)
    lane = lax.broadcasted_iota(jnp.int32, (ROWS, LANES), 1)

    def moved(tile, amount):
        return pltpu.roll(tile, amount % LANES, 1) if amount % LANES else tile

    def columns(landing, b, block):
        height = landing.shape[1]
        at = lane[:height]
        value = jnp.zeros((height, LANES), F32)
        base = block * LANES
        for t in range(base // width, min(count - 1, (base + LANES - 1) // width) + 1):
            low = width * t - base
            value = jnp.where(
                (at >= low) & (at < low + width),
                moved(landing[t], width * (t - b)),
                value,
            )
        return value

    def tile_of(values, t):
        value = jnp.zeros((ROWS, LANES), F32)
        base = width * t
        for b in range(bricks):
            for block in range(base // LANES, (base + width - 1) // LANES + 1):
                low = max(block * LANES, base) - base + b * width
                high = min((block + 1) * LANES, base + width) - base + b * width
                value = jnp.where(
                    (lane >= low) & (lane < high),
                    moved(values[b, :, pl.ds(block * LANES, LANES)], width * (b - t)),
                    value,
                )
        return value

    def forward(part):
        span = edges[part + 1] - edges[part]
        lanes = pl.ds(edges[part], span)
        lines = lax.broadcasted_iota(jnp.int32, (side, span), 0).astype(F32)
        span_row = lax.broadcasted_iota(jnp.int32, (ROWS, span), 0)
        for b in range(bricks):
            for orient in range(orients):
                near_a = jnp.maximum(
                    0.0, 1.0 - jnp.abs(spots[b, pl.ds(2 * orient, 1), lanes] - lines)
                )
                near_b = jnp.maximum(
                    0.0, 1.0 - jnp.abs(spots[b, pl.ds(2 * orient + 1, 1), lanes] - lines)
                )
                weights = near_a[:, None, :] * near_b[None, :, :]
                corner[b, pl.ds(orient * cells, cells), lanes] = weights.reshape(
                    cells, span
                ).astype(BF16)
            mixed = matmul(planes_t[b], corner[b, :, lanes], ((1,), (0,))).astype(BF16)
            feature[b, :, lanes] = mixed
            before = matmul(first_t[b], mixed, ((1,), (0,)))
            active = jnp.maximum(before, 0.0).astype(BF16)
            hidden[b, :, lanes] = active
            raw = matmul(last_wide[b].astype(BF16), active, ((1,), (0,)))
            gate = jax.nn.sigmoid(raw)
            soft = jnp.maximum(raw, 0.0) + jnp.log1p(jnp.exp(-jnp.abs(raw)))
            answers[b, :, lanes] = jnp.where(span_row == 0, soft, gate)
            slope[b, :, lanes] = jnp.where(span_row == 0, gate, gate * (1.0 - gate))

    for part in range(2):
        gather_in(0, part, out_a, in_a, reach[part], reach[part + 1])
        for b in range(bricks):
            for block in range(edges[part] // LANES, edges[part + 1] // LANES):
                spots[b, pl.ds(0, 2 * orients), pl.ds(block * LANES, LANES)] = columns(
                    in_a, b, block
                )
        forward(part)
        for t in range(ready[part], ready[part + 1]):
            out_b[t] = tile_of(answers, t)[:HALF]
        spread_out(1, part, out_b, in_b, behind, max(ready[part], 1), ready[part + 1])
    in_b[0] = out_b[0]
    sent(0, out_a, in_a)

    found = jnp.zeros((ROWS, total), F32)
    for part in range(2):
        start, stop = ready[part], ready[part + 1]
        gather_in(1, part, out_b, in_b, max(start, 1), stop)
        held = jnp.concatenate([in_b[t] for t in range(start, stop)], axis=0)
        taken = matmul(
            jnp.concatenate([value.astype(BF16) for value in parts_of(held, 2)], axis=0),
            lane_hot,
            ((1,), (0,)),
        )
        height = (stop - start) * HALF
        taken = (taken[:height] + taken[height:]).reshape(height // ROWS, ROWS, total)
        found = found + jnp.sum(jnp.where(paired(start, stop), taken, 0.0), axis=0)
    found = found[:HALF] + found[HALF:]
    found = jnp.concatenate([found, found], axis=0)
    views = [found[:, i * rays : (i + 1) * rays] for i in range(points)]
    lengths = [
        step_ref[k, pl.ds(s, 1), :] for k in range(crossed) for s in range(samples)
    ]
    running = jnp.zeros((1, rays), F32)
    colour = jnp.zeros((ROWS, rays), F32)
    weights, passed = [], []
    for i in range(points):
        depth = views[i][0:1] * lengths[i]
        weight = jnp.exp(-running) * (1.0 - jnp.exp(-depth))
        running = running + depth
        passed.append(jnp.exp(-running))
        weights.append(weight)
        colour = colour + weight * views[i]
    colour_ref[...] = colour[1:4]
    residual = jnp.where((row & 3) > 0, colour - target_tile[...], 0.0)
    behind_sum = jnp.zeros((1, rays), F32)
    cotangents = [None] * points
    for i in reversed(range(points)):
        shade_dot = jnp.sum((views[i] * residual)[:HALF], axis=0, keepdims=True)
        density_cot = (passed[i] * shade_dot - behind_sum) * lengths[i]
        behind_sum = behind_sum + weights[i] * shade_dot
        cotangents[i] = jnp.where((row & 3) == 0, density_cot, weights[i] * residual)
    cotangent_parts = parts_of(jnp.concatenate(cotangents, axis=1), 2)
    middle = count // 2
    for start, stop in ((middle, count), (0, middle)):
        tiles = scatter(cotangent_parts, paired(start, stop))
        for t in range(start, stop):
            at = t - start
            out_c[t] = tiles[at // 2, (at % 2) * HALF : (at % 2 + 1) * HALF]
        spread_out(2, 0, out_c, in_c, ahead, max(start, 1), stop)
    in_c[0] = out_c[0]
    sent(1, out_b, in_b)
    gather_in(2, 0, out_c, in_c, 1, count)
    sent(2, out_c, in_c)
    for b in range(bricks):
        for block in range(slots // LANES):
            lanes = pl.ds(block * LANES, LANES)
            pull = columns(in_c, b, block)
            raw_cot[b, :, lanes] = (
                jnp.concatenate([pull, jnp.zeros_like(pull)], axis=0) * slope[b, :, lanes]
            )


def gradient_kernel(
    colour_in, corner, feature, hidden, raw_cot, first_ref, last_wide,
    colour_out, plane_out, first_out, last_out,
    plane_part, first_part, last_part, before_cot, feature_cot, sems,
):
    bricks, _, slots = corner.shape
    colour_copy = pltpu.make_async_copy(colour_in, colour_out, sems.at[0, 3])
    colour_copy.start()

    def result_copies(b):
        pairs = ((plane_part, plane_out), (first_part, first_out), (last_part, last_out))
        return [
            pltpu.make_async_copy(source.at[b], landing.at[b], sems.at[b, at])
            for at, (source, landing) in enumerate(pairs)
        ]

    edges = column_edges(slots)
    for b in range(bricks):
        cot = raw_cot[b].astype(BF16)
        for start, stop in zip(edges, edges[1:]):
            lanes = pl.ds(start, stop - start)
            pull = matmul(last_wide[b].astype(BF16), cot[:, start:stop], ((0,), (0,)))
            masked = jnp.where(hidden[b, :, lanes].astype(F32) > 0.0, pull, 0.0).astype(BF16)
            before_cot[b, :, lanes] = masked
            feature_cot[b, :, lanes] = matmul(first_ref[b], masked, ((1,), (0,))).astype(BF16)
        plane_copy, first_copy, last_copy = result_copies(b)
        plane_part[b] = matmul(corner[b], feature_cot[b], ((1,), (1,)))
        plane_copy.start()
        first_part[b] = matmul(feature[b], before_cot[b], ((1,), (1,)))
        first_copy.start()
        last_part[b] = matmul(cot, hidden[b], ((1,), (1,)))[:HALF]
        last_copy.start()
    colour_copy.wait()
    for b in range(bricks):
        for copy in result_copies(b):
            copy.wait()


def on_device(
    along_x, along_y,
    brick_ids, cell_index, cell_frac, step_length, target, planes, first_layer, last_layer,
):
    count = along_x * along_y
    bricks, orients, cells, channels = planes.shape
    units = first_layer.shape[2]
    rays, crossed = brick_ids.shape
    samples = step_length.shape[1]
    all_bricks = bricks * count
    capacity = max(2, (3 * rays * crossed + all_bricks - 1) // all_bricks)
    width = capacity * samples
    assert bricks == 2 and bricks * width <= LANES
    assert count & (count - 1) == 0 and along_y & (along_y - 1) == 0
    slots = (count * width + CHUNK - 1) // CHUNK * CHUNK
    total = crossed * samples * rays
    flat = (bricks, orients * cells, channels)
    vmem = pl.BlockSpec(memory_space=pltpu.VMEM)
    hbm = pl.BlockSpec(memory_space=pltpu.HBM)
    wide = pltpu.VMEM((bricks, ROWS, slots), F32)
    tile = pltpu.VMEM((count, 2 * orients, LANES), F32)
    half_tile = pltpu.VMEM((count, HALF, LANES), F32)
    limit = 32 * 1024 * 1024
    inputs = (
        brick_ids.T, cell_index, cell_frac, step_length, target, last_layer, planes, first_layer
    )
    held = pl.pallas_call(
        functools.partial(step_kernel, along_x, along_y, capacity),
        out_shape=[
            pltpu.VMEM(target.shape, F32),
            pltpu.VMEM((bricks, orients * cells, slots), BF16),
            pltpu.VMEM((bricks, channels, slots), BF16),
            pltpu.VMEM((bricks, units, slots), BF16),
            pltpu.VMEM((bricks, ROWS, slots), F32),
            pltpu.VMEM(first_layer.shape, BF16),
            pltpu.VMEM((bricks, ROWS, units), F32),
        ],
        in_specs=[vmem] * 6 + [hbm] * 2,
        out_specs=[vmem] * 7,
        scratch_shapes=[
            pltpu.VMEM((ROWS, total), F32),
            pltpu.VMEM((ROWS, rays), F32),
            pltpu.VMEM(planes.shape, BF16),
            wide, wide, wide,
            tile, tile, half_tile, half_tile, half_tile, half_tile,
            pltpu.VMEM((bricks, channels, orients * cells), BF16),
            pltpu.VMEM((bricks, units, channels), BF16),
            pltpu.SemaphoreType.DMA((2,)),
            pltpu.SemaphoreType.DMA((3,)),
            pltpu.SemaphoreType.DMA((3, 2)),
        ],
        compiler_params=pltpu.CompilerParams(
            collective_id=0, has_side_effects=True, vmem_limit_bytes=limit
        ),
    )(*[pltpu.with_memory_space_constraint(value, pltpu.HBM) for value in inputs])
    colour, plane_grad, first_grad, last_grad = pl.pallas_call(
        gradient_kernel,
        out_shape=[
            jax.ShapeDtypeStruct(shape, F32)
            for shape in (target.shape, flat, first_layer.shape, last_layer.shape)
        ],
        in_specs=[vmem] * 7,
        out_specs=[hbm] * 4,
        scratch_shapes=[
            pltpu.VMEM(flat, F32),
            pltpu.VMEM(first_layer.shape, F32),
            pltpu.VMEM(last_layer.shape, F32),
            pltpu.VMEM((bricks, units, slots), BF16),
            pltpu.VMEM((bricks, channels, slots), BF16),
            pltpu.SemaphoreType.DMA((bricks, 4)),
        ],
        compiler_params=pltpu.CompilerParams(vmem_limit_bytes=limit),
    )(*[pltpu.with_memory_space_constraint(value, pltpu.VMEM) for value in held])
    return colour, plane_grad.reshape(planes.shape), first_grad, last_grad


def solution(mesh):
    along_x, along_y = mesh.shape["bx"], mesh.shape["by"]
    return jax.shard_map(
        functools.partial(on_device, along_x, along_y),
        mesh=mesh,
        in_specs=(
            P(("bx", "by"), None),
            P(None, None, None, ("bx", "by")),
            P(None, None, None, ("bx", "by")),
            P(None, None, ("bx", "by")),
            P(None, ("bx", "by")),
            P(("bx", "by"), None, None, None),
            P(("bx", "by"), None, None),
            P(("bx", "by"), None, None),
        ),
        out_specs=(
            P(None, ("bx", "by")),
            P(("bx", "by"), None, None, None),
            P(("bx", "by"), None, None),
            P(("bx", "by"), None, None),
        ),
        check_vma=False,
    )
```

```python
import functools

import jax
import jax.numpy as jnp
from jax import lax
from jax.experimental import pallas as pl
from jax.experimental.pallas import tpu as pltpu
from jax.sharding import PartitionSpec as P

MESH = pl.DeviceIdType.MESH
F32 = jnp.float32
BF16 = jnp.bfloat16
LANES = 128
ROWS = 8
CHUNK = 256
HALF = 4


def matmul(lhs, rhs, contract):
    return lax.dot_general(lhs, rhs, (contract, ((), ())), preferred_element_type=F32)


def parts_of(value, number):
    parts = []
    for _ in range(number - 1):
        part = value.astype(BF16).astype(F32)
        parts.append(part)
        value = value - part
    return parts + [value]


def column_edges(slots):
    first = (slots // 2 + CHUNK - 1) // CHUNK * CHUNK
    return [0, first, slots]


def step_kernel(
    along_x, along_y, capacity,
    ids_ref, cell_ref, frac_ref, step_ref, target_ref, last_ref, planes_hbm, first_hbm,
    colour_ref, corner, feature, hidden, raw_cot, first_ref, last_wide,
    payload, target_tile, planes_ref, spots, answers, slope,
    out_a, in_a, out_b, in_b, out_c, in_c,
    planes_t, first_t,
    load_sem, send_sem, recv_sem,
):
    count = along_x * along_y
    bricks, orients, cells, channels = planes_ref.shape
    side = 1
    while side * side < cells:
        side = side * 2
    crossed, samples, rays = step_ref.shape
    points = crossed * samples
    total = points * rays
    segments = crossed * rays
    width = capacity * samples
    slots = corner.shape[2]
    all_bricks = bricks * count
    me = lax.axis_index("bx") * along_y + lax.axis_index("by")

    load_planes = pltpu.make_async_copy(planes_hbm, planes_ref, load_sem.at[0])
    load_first = pltpu.make_async_copy(first_hbm, first_ref, load_sem.at[1])

    shift_y = along_y.bit_length() - 1

    def device(number):
        number = number & (count - 1)
        return (lax.shift_right_logical(number, shift_y), number & (along_y - 1))

    def ahead(offset):
        return device(me + offset)

    def behind(offset):
        return device(me + count - offset)

    def transfer(phase, part, source, landing, where, peer):
        return pltpu.make_async_remote_copy(
            src_ref=source.at[where],
            dst_ref=landing.at[where],
            send_sem=send_sem.at[phase],
            recv_sem=recv_sem.at[phase, part],
            device_id=peer,
            device_id_type=MESH,
        )

    def spread_out(phase, part, source, landing, peer, start, stop):
        def send(offset, carry):
            transfer(phase, part, source, landing, offset, peer(offset)).start()
            return carry

        lax.fori_loop(start, stop, send, 0, unroll=True)

    def gather_in(phase, part, source, landing, start, stop):
        rows = pl.ds(start, stop - start)
        transfer(phase, part, source, landing, rows, ahead(1)).wait_recv()

    def sent(phase, source, landing):
        transfer(phase, 0, source, landing, pl.ds(1, count - 1), ahead(1)).wait_send()

    barrier = pltpu.get_barrier_semaphore()

    def greet(offset, carry):
        pl.semaphore_signal(barrier, inc=1, device_id=ahead(offset), device_id_type=MESH)
        return carry

    lax.fori_loop(1, count, greet, 0, unroll=True)
    load_planes.start()
    load_first.start()

    ids = [ids_ref[pl.ds(k, 1), :] for k in range(crossed)]
    ids_row = jnp.concatenate(ids, axis=1)
    member = lax.broadcasted_iota(jnp.int32, (all_bricks, segments), 0) == ids_row
    member_f = jnp.where(member, 1.0, 0.0).astype(F32)
    earlier = lax.broadcasted_iota(jnp.int32, (segments, segments), 0) < lax.broadcasted_iota(
        jnp.int32, (segments, segments), 1
    )
    ranks = matmul(
        member_f.astype(BF16), jnp.where(earlier, 1.0, 0.0).astype(BF16), ((1,), (0,))
    )
    ranking = jnp.sum(member_f * ranks, axis=0, keepdims=True).astype(jnp.int32)
    shift = bricks.bit_length() - 1
    away = lax.shift_right_logical(ids_row, shift) - me
    away = jnp.where(away < 0, away + count, away)
    place = (ids_row & (bricks - 1)) * width + ranking
    away_all, place_all = [], []
    for k in range(crossed):
        block = slice(k * rays, (k + 1) * rays)
        for s in range(samples):
            away_all.append(away[:, block])
            place_all.append(place[:, block] + s * capacity)
    away_all = jnp.concatenate(away_all, axis=1)
    place_all = jnp.concatenate(place_all, axis=1)
    lane_hot = jnp.where(
        lax.broadcasted_iota(jnp.int32, (LANES, total), 0) == place_all, 1.0, 0.0
    ).astype(BF16)
    def whole(start, stop):
        shape = (stop - start, ROWS, total)
        return lax.broadcasted_iota(jnp.int32, shape, 0) + start == away_all[None]

    def paired(start, stop):
        shape = ((stop - start) // 2, ROWS, total)
        return (
            2 * lax.broadcasted_iota(jnp.int32, shape, 0)
            + lax.shift_right_logical(lax.broadcasted_iota(jnp.int32, shape, 1), 2)
            + start
        ) == away_all[None]

    def scatter(parts, chosen):
        tiles = chosen.shape[0]
        height = tiles * ROWS
        spread = jnp.concatenate(
            [
                jnp.where(chosen, part[None], 0.0).reshape(height, total).astype(BF16)
                for part in parts
            ],
            axis=0,
        )
        placed = matmul(spread, lane_hot, ((1,), (1,)))
        merged = placed[:height]
        for at in range(1, len(parts)):
            merged = merged + placed[at * height : (at + 1) * height]
        return merged.reshape(tiles, ROWS, LANES)

    payload[...] = jnp.zeros_like(payload)
    for k in range(crossed):
        for s in range(samples):
            lanes = pl.ds((k * samples + s) * rays, rays)
            for axis in range(2 * orients):
                payload[pl.ds(axis, 1), lanes] = (
                    cell_ref[axis, k, pl.ds(s, 1), :].astype(F32)
                    + frac_ref[axis, k, pl.ds(s, 1), :]
                )
    edges = column_edges(slots)
    reach = [1] + [min(count, (stop - 1) // width + 1) for stop in edges[1:]]
    ready = [0, edges[1] // width // 4 * 4, count]
    payload_parts = parts_of(payload[...], 3)
    for part in range(2):
        start, stop = (0, reach[1]) if part == 0 else (reach[1], count)
        tiles = scatter(payload_parts, whole(start, stop))
        out_a[pl.ds(start, stop - start)] = tiles[:, : 2 * orients]
        if part == 0:
            in_a[0] = tiles[0, : 2 * orients]
            pl.semaphore_wait(barrier, count - 1)
        spread_out(0, part, out_a, in_a, ahead, max(start, 1), stop)

    load_planes.wait()
    load_first.wait()
    for b in range(bricks):
        for orient in range(orients):
            planes_t[b, :, pl.ds(orient * cells, cells)] = planes_ref[b, orient].T
        first_t[b] = first_ref[b].T
    last_wide[...] = jnp.zeros_like(last_wide)
    for b in range(bricks):
        last_wide[b, pl.ds(0, HALF), :] = last_ref[b].astype(F32)
    target_tile[...] = jnp.zeros_like(target_tile)
    target_tile[pl.ds(1, 3), :] = target_ref[...]
    target_tile[pl.ds(HALF + 1, 3), :] = target_ref[...]

    row = lax.broadcasted_iota(jnp.int32, (ROWS, LANES), 0)
    lane = lax.broadcasted_iota(jnp.int32, (ROWS, LANES), 1)

    def moved(tile, amount):
        return pltpu.roll(tile, amount % LANES, 1) if amount % LANES else tile

    def columns(landing, b, block):
        height = landing.shape[1]
        at = lane[:height]
        value = jnp.zeros((height, LANES), F32)
        base = block * LANES
        for t in range(base // width, min(count - 1, (base + LANES - 1) // width) + 1):
            low = width * t - base
            value = jnp.where(
                (at >= low) & (at < low + width),
                moved(landing[t], width * (t - b)),
                value,
            )
        return value

    def tile_of(values, t):
        value = jnp.zeros((ROWS, LANES), F32)
        base = width * t
        for b in range(bricks):
            for block in range(base // LANES, (base + width - 1) // LANES + 1):
                low = max(block * LANES, base) - base + b * width
                high = min((block + 1) * LANES, base + width) - base + b * width
                value = jnp.where(
                    (lane >= low) & (lane < high),
                    moved(values[b, :, pl.ds(block * LANES, LANES)], width * (b - t)),
                    value,
                )
        return value

    def forward(part):
        span = edges[part + 1] - edges[part]
        lanes = pl.ds(edges[part], span)
        lines = lax.broadcasted_iota(jnp.int32, (side, span), 0).astype(F32)
        span_row = lax.broadcasted_iota(jnp.int32, (ROWS, span), 0)
        for b in range(bricks):
            for orient in range(orients):
                near_a = jnp.maximum(
                    0.0, 1.0 - jnp.abs(spots[b, pl.ds(2 * orient, 1), lanes] - lines)
                )
                near_b = jnp.maximum(
                    0.0, 1.0 - jnp.abs(spots[b, pl.ds(2 * orient + 1, 1), lanes] - lines)
                )
                weights = near_a[:, None, :] * near_b[None, :, :]
                corner[b, pl.ds(orient * cells, cells), lanes] = weights.reshape(
                    cells, span
                ).astype(BF16)
            mixed = matmul(planes_t[b], corner[b, :, lanes], ((1,), (0,))).astype(BF16)
            feature[b, :, lanes] = mixed
            before = matmul(first_t[b], mixed, ((1,), (0,)))
            active = jnp.maximum(before, 0.0).astype(BF16)
            hidden[b, :, lanes] = active
            raw = matmul(last_wide[b].astype(BF16), active, ((1,), (0,)))
            gate = jax.nn.sigmoid(raw)
            soft = jnp.maximum(raw, 0.0) + jnp.log1p(jnp.exp(-jnp.abs(raw)))
            answers[b, :, lanes] = jnp.where(span_row == 0, soft, gate)
            slope[b, :, lanes] = jnp.where(span_row == 0, gate, gate * (1.0 - gate))

    for part in range(2):
        gather_in(0, part, out_a, in_a, reach[part], reach[part + 1])
        for b in range(bricks):
            for block in range(edges[part] // LANES, edges[part + 1] // LANES):
                spots[b, pl.ds(0, 2 * orients), pl.ds(block * LANES, LANES)] = columns(
                    in_a, b, block
                )
        forward(part)
        for t in range(ready[part], ready[part + 1]):
            out_b[t] = tile_of(answers, t)[:HALF]
        spread_out(1, part, out_b, in_b, behind, max(ready[part], 1), ready[part + 1])
    in_b[0] = out_b[0]
    sent(0, out_a, in_a)

    found = jnp.zeros((ROWS, total), F32)
    for part in range(2):
        start, stop = ready[part], ready[part + 1]
        gather_in(1, part, out_b, in_b, max(start, 1), stop)
        held = jnp.concatenate([in_b[t] for t in range(start, stop)], axis=0)
        taken = matmul(
            jnp.concatenate([value.astype(BF16) for value in parts_of(held, 2)], axis=0),
            lane_hot,
            ((1,), (0,)),
        )
        height = (stop - start) * HALF
        taken = (taken[:height] + taken[height:]).reshape(height // ROWS, ROWS, total)
        found = found + jnp.sum(jnp.where(paired(start, stop), taken, 0.0), axis=0)
    found = found[:HALF] + found[HALF:]
    found = jnp.concatenate([found, found], axis=0)
    views = [found[:, i * rays : (i + 1) * rays] for i in range(points)]
    lengths = [
        step_ref[k, pl.ds(s, 1), :] for k in range(crossed) for s in range(samples)
    ]
    running = jnp.zeros((1, rays), F32)
    colour = jnp.zeros((ROWS, rays), F32)
    weights, passed = [], []
    for i in range(points):
        depth = views[i][0:1] * lengths[i]
        weight = jnp.exp(-running) * (1.0 - jnp.exp(-depth))
        running = running + depth
        passed.append(jnp.exp(-running))
        weights.append(weight)
        colour = colour + weight * views[i]
    colour_ref[...] = colour[1:4]
    residual = jnp.where((row & 3) > 0, colour - target_tile[...], 0.0)
    behind_sum = jnp.zeros((1, rays), F32)
    cotangents = [None] * points
    for i in reversed(range(points)):
        shade_dot = jnp.sum((views[i] * residual)[:HALF], axis=0, keepdims=True)
        density_cot = (passed[i] * shade_dot - behind_sum) * lengths[i]
        behind_sum = behind_sum + weights[i] * shade_dot
        cotangents[i] = jnp.where((row & 3) == 0, density_cot, weights[i] * residual)
    cotangent_parts = parts_of(jnp.concatenate(cotangents, axis=1), 2)
    middle = count // 2
    for start, stop in ((middle, count), (0, middle)):
        tiles = scatter(cotangent_parts, paired(start, stop))
        for t in range(start, stop):
            at = t - start
            out_c[t] = tiles[at // 2, (at % 2) * HALF : (at % 2 + 1) * HALF]
        spread_out(2, 0, out_c, in_c, ahead, max(start, 1), stop)
    in_c[0] = out_c[0]
    sent(1, out_b, in_b)
    gather_in(2, 0, out_c, in_c, 1, count)
    sent(2, out_c, in_c)
    for b in range(bricks):
        for block in range(slots // LANES):
            lanes = pl.ds(block * LANES, LANES)
            pull = columns(in_c, b, block)
            raw_cot[b, :, lanes] = (
                jnp.concatenate([pull, jnp.zeros_like(pull)], axis=0) * slope[b, :, lanes]
            )


def gradient_kernel(
    colour_in, corner, feature, hidden, raw_cot, first_ref, last_wide,
    colour_out, plane_out, first_out, last_out,
    plane_part, first_part, last_part, before_cot, feature_cot, sems,
):
    bricks, _, slots = corner.shape
    colour_copy = pltpu.make_async_copy(colour_in, colour_out, sems.at[0, 3])
    colour_copy.start()

    def result_copies(b):
        pairs = ((plane_part, plane_out), (first_part, first_out), (last_part, last_out))
        return [
            pltpu.make_async_copy(source.at[b], landing.at[b], sems.at[b, at])
            for at, (source, landing) in enumerate(pairs)
        ]

    edges = column_edges(slots)
    for b in range(bricks):
        cot = raw_cot[b].astype(BF16)
        for start, stop in zip(edges, edges[1:]):
            lanes = pl.ds(start, stop - start)
            pull = matmul(last_wide[b].astype(BF16), cot[:, start:stop], ((0,), (0,)))
            masked = jnp.where(hidden[b, :, lanes].astype(F32) > 0.0, pull, 0.0).astype(BF16)
            before_cot[b, :, lanes] = masked
            feature_cot[b, :, lanes] = matmul(first_ref[b], masked, ((1,), (0,))).astype(BF16)
        plane_copy, first_copy, last_copy = result_copies(b)
        plane_part[b] = matmul(corner[b], feature_cot[b], ((1,), (1,)))
        plane_copy.start()
        first_part[b] = matmul(feature[b], before_cot[b], ((1,), (1,)))
        first_copy.start()
        last_part[b] = matmul(cot, hidden[b], ((1,), (1,)))[:HALF]
        last_copy.start()
    colour_copy.wait()
    for b in range(bricks):
        for copy in result_copies(b):
            copy.wait()


def on_device(
    along_x, along_y,
    brick_ids, cell_index, cell_frac, step_length, target, planes, first_layer, last_layer,
):
    count = along_x * along_y
    bricks, orients, cells, channels = planes.shape
    units = first_layer.shape[2]
    rays, crossed = brick_ids.shape
    samples = step_length.shape[1]
    all_bricks = bricks * count
    capacity = max(2, (3 * rays * crossed + all_bricks - 1) // all_bricks)
    width = capacity * samples
    assert bricks == 2 and bricks * width <= LANES
    assert count & (count - 1) == 0 and along_y & (along_y - 1) == 0
    slots = (count * width + CHUNK - 1) // CHUNK * CHUNK
    total = crossed * samples * rays
    flat = (bricks, orients * cells, channels)
    vmem = pl.BlockSpec(memory_space=pltpu.VMEM)
    hbm = pl.BlockSpec(memory_space=pltpu.HBM)
    wide = pltpu.VMEM((bricks, ROWS, slots), F32)
    tile = pltpu.VMEM((count, 2 * orients, LANES), F32)
    half_tile = pltpu.VMEM((count, HALF, LANES), F32)
    limit = 32 * 1024 * 1024
    inputs = (
        brick_ids.T, cell_index, cell_frac, step_length, target, last_layer, planes, first_layer
    )
    held = pl.pallas_call(
        functools.partial(step_kernel, along_x, along_y, capacity),
        out_shape=[
            pltpu.VMEM(target.shape, F32),
            pltpu.VMEM((bricks, orients * cells, slots), BF16),
            pltpu.VMEM((bricks, channels, slots), BF16),
            pltpu.VMEM((bricks, units, slots), BF16),
            pltpu.VMEM((bricks, ROWS, slots), F32),
            pltpu.VMEM(first_layer.shape, BF16),
            pltpu.VMEM((bricks, ROWS, units), F32),
        ],
        in_specs=[vmem] * 6 + [hbm] * 2,
        out_specs=[vmem] * 7,
        scratch_shapes=[
            pltpu.VMEM((ROWS, total), F32),
            pltpu.VMEM((ROWS, rays), F32),
            pltpu.VMEM(planes.shape, BF16),
            wide, wide, wide,
            tile, tile, half_tile, half_tile, half_tile, half_tile,
            pltpu.VMEM((bricks, channels, orients * cells), BF16),
            pltpu.VMEM((bricks, units, channels), BF16),
            pltpu.SemaphoreType.DMA((2,)),
            pltpu.SemaphoreType.DMA((3,)),
            pltpu.SemaphoreType.DMA((3, 2)),
        ],
        compiler_params=pltpu.CompilerParams(
            collective_id=0, has_side_effects=True, vmem_limit_bytes=limit
        ),
    )(*[pltpu.with_memory_space_constraint(value, pltpu.HBM) for value in inputs])
    colour, plane_grad, first_grad, last_grad = pl.pallas_call(
        gradient_kernel,
        out_shape=[
            jax.ShapeDtypeStruct(shape, F32)
            for shape in (target.shape, flat, first_layer.shape, last_layer.shape)
        ],
        in_specs=[vmem] * 7,
        out_specs=[hbm] * 4,
        scratch_shapes=[
            pltpu.VMEM(flat, F32),
            pltpu.VMEM(first_layer.shape, F32),
            pltpu.VMEM(last_layer.shape, F32),
            pltpu.VMEM((bricks, units, slots), BF16),
            pltpu.VMEM((bricks, channels, slots), BF16),
            pltpu.SemaphoreType.DMA((bricks, 4)),
        ],
        compiler_params=pltpu.CompilerParams(vmem_limit_bytes=limit),
    )(*[pltpu.with_memory_space_constraint(value, pltpu.VMEM) for value in held])
    return colour, plane_grad.reshape(planes.shape), first_grad, last_grad


def solution(mesh):
    along_x, along_y = mesh.shape["bx"], mesh.shape["by"]
    return jax.shard_map(
        functools.partial(on_device, along_x, along_y),
        mesh=mesh,
        in_specs=(
            P(("bx", "by"), None),
            P(None, None, None, ("bx", "by")),
            P(None, None, None, ("bx", "by")),
            P(None, None, ("bx", "by")),
            P(None, ("bx", "by")),
            P(("bx", "by"), None, None, None),
            P(("bx", "by"), None, None),
            P(("bx", "by"), None, None),
        ),
        out_specs=(
            P(None, ("bx", "by")),
            P(("bx", "by"), None, None, None),
            P(("bx", "by"), None, None),
            P(("bx", "by"), None, None),
        ),
        check_vma=False,
    )
```
